512 devices in a mesh: ctx: 16 (over z_hi, x, core), exp: 32 (over z_lo, y).
Axes of the slice: x: 4, y: 8, z: 8 (z_hi: 2, z_lo: 4; z = z_hi * 4 + z_lo), core: 2. Of those that a mesh axis runs over, the one named last changes fastest.
Arguments:
- queries: bfloat16 [8192, 8192], P('ctx', 'exp'), may hold values from -80 to 80
- key_states: bfloat16 [8192, 512], P('ctx'), may hold values from -4 to 4
- value_states: bfloat16 [8192, 512], P('ctx'), may hold values from -6 to 6
- token_states: bfloat16 [2048, 4096], P('exp', 'ctx'), may hold values from -6 to 6
- expert_ids: int32 [2048, 8], P('exp'), may hold values from 0 to 31, all different within a row; in each aligned block of 64 rows (0 to 63, 64 to 127, ...) at most 18 rows name the same one
- combine_weights: float32 [2048, 8], P('exp'), may hold values from 0.1 to 1
- gate_weight: bfloat16 [32, 4096, 1536], P('exp', 'ctx'), may hold values from -0.09375 to 0.09375
- up_weight: bfloat16 [32, 4096, 1536], P('exp', 'ctx'), may hold values from -0.09375 to 0.09375
- down_weight: bfloat16 [32, 1536, 4096], P('exp', None, 'ctx'), may hold values from -0.15625 to 0.15625
Outputs:
- context: bfloat16 [8192, 8192], P('ctx', 'exp')
- moe_output: bfloat16 [2048, 4096], P('exp', 'ctx')
The draws below stay inside these ranges and needn't reach their ends.
Inputs may be any that keep to these rules, and one draw needn't show every extreme that they name: `expert_ids`: each row names 8 different experts. Within each aligned block of 64 rows (the tokens of one device) no expert is named by more than 18 rows, and in every draw some expert is named by exactly 18 rows of some block.
All inputs are finite; a program needn't handle non-finite values.
Results may differ from the reference program's by a relative error of at most 0.011.
Values may be sent and summed in bfloat16 or wider, within the bound.
No kernel may reach another device: no remote copies, remote signals or barrier semaphores. Data moves between devices by JAX's collectives and lax.ppermute only.
A program may use at most 64 MiB of HBM per device.

```python
import math
import jax
import jax.numpy as jnp
import numpy as np
from jax import lax

D = 4096
FF = 1536
HEADS = 64
KVH = 4
HD = 128
TOPK = 8
EXPERTS = 32
TOK_DEV = 64
CAP = 18
SEQ = 8192
TOKENS = 2048
N_CTX = 16
N_EXP = 32


def shared_keys(key):
    drawn = jax.random.normal(key, (SEQ, KVH * HD), jnp.float32)
    return jnp.clip(drawn, -4.0, 4.0)


def draw_key_states(key, part):
    base_keys = shared_keys(key)
    return base_keys.astype(jnp.bfloat16)


def draw_queries(key, part):
    key = jax.random.fold_in(key, 2)
    drawn = jnp.clip(jax.random.normal(key, (SEQ, HEADS * HD), jnp.float32), -4.0, 4.0)
    return drawn.astype(jnp.bfloat16)


def block_levels(key, shape, shards, least, largest):
    gain, own = 1.0, jax.random.fold_in(key, 6)
    for dim, shards_of in shards:
        draws = jnp.exp(jax.random.uniform(jax.random.fold_in(own, dim), (shards_of,), jnp.float32, least / len(shards), largest / len(shards)))
        gain = gain * jnp.repeat(draws, shape[dim] // shards_of).reshape([-1 if axis == dim else 1 for axis in range(len(shape))])
    return gain


def routed_block(own_key, own, number, rows, number_of, top, reach, skew):
    sequence = jax.random.permutation(own_key, number_of)
    heavy_load, ordinary = shares(number_of, rows * top, reach, skew, True), shares(number_of, rows * top, reach, skew, False)
    places = jnp.arange(number_of)

    def named(tallies, rotation):
        used = int((tallies > 0).sum())
        fixed = max(1, used // 4)
        moved = fixed + (places - fixed + rotation * (used - fixed)) % max(1, number_of - fixed)
        return jnp.zeros((number_of,), jnp.int32).at[sequence[jnp.where(places < fixed, places, moved)]].set(jnp.asarray(tallies, jnp.int32))

    tallies = jnp.where(number % 4 == 0, named(heavy_load, number // 4), named(ordinary, number - number // 4 - 1))
    mixed = jax.random.permutation(jax.random.fold_in(own, 3), number_of)
    giver, taker = mixed[0:number_of // 2 * 2:2], mixed[1:number_of // 2 * 2:2]
    margin = jnp.minimum(tallies[giver] - 1, reach - tallies[taker]) // 2
    margin = jnp.where((giver == sequence[0]) | (taker == sequence[0]) | (tallies[taker] == 0), 0, jnp.maximum(margin, 0))
    moved = jax.random.randint(jax.random.fold_in(own, 4), (number_of // 2,), 0, 1 << 20) % (margin + 1)
    tallies = tallies.at[giver].add(-moved).at[taker].add(moved)
    labels = jnp.searchsorted(jnp.cumsum(tallies), jnp.arange(rows * top), side="right").astype(jnp.int32)
    listing = labels.reshape(top, rows).T
    listing = listing[jax.random.permutation(jax.random.fold_in(own, 1), rows)]
    rotation = jax.random.randint(jax.random.fold_in(own, 2), (rows, 1), 0, top)
    return jnp.take_along_axis(listing, (jnp.arange(top)[None, :] + rotation) % top, axis=1)


def shares(number_of, total, most, slope, full):
    weights = [(1 << 20) // math.isqrt(standing ** slope) + 1 for standing in range(1, number_of + 1)]
    largest = most if full else min(most, max(-(-total // number_of), total * weights[0] // sum(weights)))
    least = 1 if total - largest >= number_of - 1 else 0
    given, spare = [largest] + [least] * (number_of - 1), total - largest - least * (number_of - 1)
    while spare > 0:
        movable = [i for i in range(1, number_of) if given[i] < largest] or [i for i in range(1, number_of) if given[i] < most]
        whole, budget = sum([weights[i] for i in movable]), spare
        for i in movable:
            more = min(most - given[i], max(1, budget * weights[i] // whole), spare)
            given[i] = given[i] + more
            spare = spare - more
    return np.array(given)


def normal_values(key, extent, spread, most, shards=(), kind=jnp.bfloat16):
    values = spread * jax.random.normal(key, extent, jnp.float32)
    if shards:
        values = values * block_levels(key, extent, shards, -0.22, 0.18)
    return jnp.clip(values, -most, most).astype(kind)


def setup_inputs(seed: int = 0) -> dict:
    seeds = jax.random.split(jax.random.key(seed), 10)
    queries = draw_queries(jax.random.fold_in(seeds[9], 71), 0)
    key_states = draw_key_states(jax.random.fold_in(seeds[9], 71), 0)
    value_states = normal_values(seeds[2], (SEQ, KVH * HD), 1.0, 6.0, ((0, 16),))
    token_states = normal_values(seeds[3], (TOKENS, D), 1.0, 6.0, ((0, 32), (1, 16)))
    expert_ids_keys = jax.random.split(jax.random.fold_in(seeds[4], 1), TOKENS // TOK_DEV)
    expert_ids_turns = jax.random.permutation(jax.random.fold_in(seeds[4], 3), TOKENS // TOK_DEV)
    expert_ids = jax.vmap(lambda own, number: routed_block(jax.random.fold_in(seeds[4], 2), own, number, TOK_DEV, EXPERTS, TOPK, CAP, 2))(expert_ids_keys, expert_ids_turns).reshape((TOKENS, TOPK))
    combine_weights = jnp.clip(jnp.exp(math.log(1.0) - 2.3025851 * jax.random.uniform(seeds[5], (TOKENS, TOPK), jnp.float32) ** block_levels(seeds[5], (TOKENS, TOPK), ((0, 32),), -0.2, 0.2)), 0.1, 1.0)
    gate_weight = normal_values(seeds[6], (EXPERTS, D, FF), D ** -0.5, 0.09375, ((0, 32), (1, 16)))
    up_weight = normal_values(seeds[7], (EXPERTS, D, FF), D ** -0.5, 0.09375, ((0, 32), (1, 16)))
    down_weight = normal_values(seeds[8], (EXPERTS, FF, D), FF ** -0.5, 0.15625, ((0, 32), (2, 16)))
    return {"queries": queries, "key_states": key_states, "value_states": value_states, "token_states": token_states, "expert_ids": expert_ids, "combine_weights": combine_weights, "gate_weight": gate_weight, "up_weight": up_weight, "down_weight": down_weight}


def head_context(query_head, key_head, value_head):
    block_rows = math.gcd(512, SEQ)
    key_pos = jnp.arange(SEQ, dtype=jnp.int32)

    def one_block(block_index):
        offset = block_index * block_rows
        query_slab = lax.dynamic_slice_in_dim(query_head, offset, block_rows, 0)
        scores = jnp.dot(query_slab, key_head.T, preferred_element_type=jnp.float32) * (HD ** -0.5)
        query_pos = offset + jnp.arange(block_rows, dtype=jnp.int32)
        allowed = query_pos[:, None] >= key_pos[None, :]
        row_peak = jnp.max(jnp.where(allowed, scores, -jnp.inf), axis=1, keepdims=True)
        weights = jnp.where(allowed, jnp.exp(scores - row_peak), 0.0)
        row_total = jnp.sum(weights, axis=1, keepdims=True)
        mixture = jnp.dot(weights.astype(jnp.bfloat16), value_head, preferred_element_type=jnp.float32)
        return (mixture / row_total).astype(jnp.bfloat16)

    blocks = lax.map(one_block, jnp.arange(SEQ // block_rows, dtype=jnp.int32))
    return blocks.reshape(SEQ, HD)


def sliced_product(picked, matrix):
    width_slice = D // N_CTX
    left = picked.reshape(picked.shape[0], N_CTX, width_slice).astype(jnp.float32)
    right = matrix.reshape(N_CTX, width_slice, FF).astype(jnp.float32)
    slices = jnp.einsum("rcd,cdf->crf", left, right).astype(jnp.bfloat16)
    slices = lax.optimization_barrier(slices)
    return jnp.sum(slices.astype(jnp.float32), axis=0)


def reference(queries, key_states, value_states, token_states, expert_ids, combine_weights, gate_weight, up_weight, down_weight):
    group_size = HEADS // KVH

    def one_head(head_index):
        query_head = lax.dynamic_slice_in_dim(queries, head_index * HD, HD, 1)
        kv_offset = (head_index // group_size) * HD
        key_head = lax.dynamic_slice_in_dim(key_states, kv_offset, HD, 1)
        value_head = lax.dynamic_slice_in_dim(value_states, kv_offset, HD, 1)
        return head_context(query_head, key_head, value_head)

    heads_out = lax.map(one_head, jnp.arange(HEADS, dtype=jnp.int32))
    context = jnp.transpose(heads_out, (1, 0, 2)).reshape(SEQ, HEADS * HD)
    row_room = N_EXP * CAP

    def one_expert(running, inputs):
        expert_index, gate_matrix, up_matrix, down_matrix = inputs
        chosen = jnp.any(expert_ids == expert_index, axis=1)
        rows = jnp.nonzero(chosen, size=row_room, fill_value=TOKENS)[0].astype(jnp.int32)
        picked = token_states.at[rows].get(mode="fill", fill_value=0)
        gate_part = sliced_product(picked, gate_matrix)
        up_part = sliced_product(picked, up_matrix)
        hidden = (jax.nn.silu(gate_part) * up_part).astype(jnp.bfloat16)
        result = jnp.dot(hidden, down_matrix, preferred_element_type=jnp.float32).astype(jnp.bfloat16)
        share = jnp.sum(jnp.where(expert_ids == expert_index, combine_weights, 0.0), axis=1)
        share_rows = share.at[rows].get(mode="fill", fill_value=0.0)
        running = running.at[rows].add(share_rows[:, None] * result.astype(jnp.float32), mode="drop")
        return running, None

    initial = jnp.zeros((TOKENS, D), jnp.float32)
    summed, unused = lax.scan(one_expert, initial, (jnp.arange(EXPERTS, dtype=jnp.int32), gate_weight, up_weight, down_weight))
    return context, summed.astype(jnp.bfloat16)
```

```python
import functools

import jax
import jax.numpy as jnp
from jax import lax
from jax.experimental import pallas as pl
from jax.experimental.pallas import tpu as pltpu
from jax.sharding import Mesh
from jax.sharding import PartitionSpec as P

FF = 1536
HALF = FF // 2
HEADS = 64
KVH = 4
HD = 128
TOPK = 8
EXPERTS = 32
CAP = 18
ROOM = 24
ROWS = EXPERTS * CAP
F32 = jnp.float32
BF16 = jnp.bfloat16
CONTRACT_LAST = (((1,), (1,)), ((), ()))
CONTRACT_FIRST = (((0,), (0,)), ((), ()))
SMEM = pl.BlockSpec(memory_space=pltpu.SMEM)
VMEM = pl.BlockSpec(memory_space=pltpu.VMEM)


def call(kernel, outs, ins, flops, moved, limit=32, scratch=(), transcendentals=0, name=None):
    return pl.pallas_call(
        kernel,
        out_shape=outs,
        in_specs=[SMEM] + [VMEM] * (len(ins) - 1),
        out_specs=jax.tree.map(lambda _: VMEM, outs),
        scratch_shapes=scratch,
        compiler_params=pltpu.CompilerParams(vmem_limit_bytes=limit << 20),
        cost_estimate=pl.CostEstimate(
            flops=flops, bytes_accessed=moved, transcendentals=transcendentals
        ),
        name=name,
    )(*ins)


def shape(dims, dtype=BF16):
    return jax.ShapeDtypeStruct(dims, dtype)


def attention_kernel(place, q_ref, kv_ref, o_ref, q2, peak, acc, *, tile, keys):
    rows, heads = q_ref.shape[0], q_ref.shape[1] // HD
    shard = place[0]
    unit = 1.4426950408889634 * HD**-0.5
    for h in range(heads):
        q = q_ref[:, h * HD : (h + 1) * HD].astype(F32) * unit
        high = q.astype(BF16)
        q2[h * rows : (h + 1) * rows, :HD] = high
        q2[h * rows : (h + 1) * rows, HD:] = (q - high.astype(F32)).astype(BF16)

    def block(start, first):
        k = kv_ref[pl.ds(start, keys), :HD]
        v = kv_ref[pl.ds(start, keys), HD:]
        kk = jnp.concatenate([k, k], axis=1)
        v1 = jnp.concatenate([v, jnp.ones_like(v)], axis=1)
        for t in range(rows * heads // tile):
            sl = slice(t * tile, (t + 1) * tile)
            s = lax.dot_general(q2[sl, :], kk, CONTRACT_LAST, preferred_element_type=F32)
            if first:
                query = (t * tile) % rows + lax.broadcasted_iota(jnp.int32, (tile, keys), 0)
                key = lax.broadcasted_iota(jnp.int32, (tile, keys), 1)
                s = jnp.where(query >= key, s, -1e30)
            new = jnp.max(s, axis=1, keepdims=True)
            if not first:
                old = peak[sl, :1]
                new = jnp.maximum(old, new)
            peak[sl, :] = jnp.broadcast_to(new, (tile, HD))
            mixed = jnp.dot(jnp.exp2(s - new).astype(BF16), v1, preferred_element_type=F32)
            acc[sl, :] = mixed if first else acc[sl, :] * jnp.exp2(old - new) + mixed

    block(pl.multiple_of(shard * rows, rows), True)

    def earlier(j, carry):
        block(pl.multiple_of(j * keys, keys), False)
        return carry

    lax.fori_loop(0, shard * (rows // keys), earlier, 0)
    for h in range(heads):
        a = acc[h * rows : (h + 1) * rows, :]
        o_ref[:, h * HD : (h + 1) * HD] = (a[:, :HD] / a[:, HD:]).astype(o_ref.dtype)


def attention(place, q, kv):
    rows, cols = q.shape
    stacked = rows * cols // HD
    return call(
        functools.partial(attention_kernel, tile=256, keys=rows),
        shape(q.shape),
        (place, q, kv),
        flops=4 * stacked * kv.shape[0] * HD,
        moved=5 << 20,
        limit=40,
        transcendentals=stacked * kv.shape[0],
        scratch=[
            pltpu.VMEM((stacked, 2 * HD), BF16),
            pltpu.VMEM((stacked, HD), F32),
            pltpu.VMEM((stacked, 2 * HD), F32),
        ],
        name="attention",
    )


def dispatch_kernel(place, ids_ref, w_ref, tokens_ref, out_ref, combine_ref):
    ids, w = ids_ref[...], w_ref[...]
    count = ids.shape[0]
    expert = lax.broadcasted_iota(jnp.int32, (count, EXPERTS), 1)
    weight = jnp.zeros((count, EXPERTS), F32)
    chosen = jnp.zeros((count, EXPERTS), F32)
    for k in range(TOPK):
        hit = ids[:, k : k + 1] == expert
        weight = weight + jnp.where(hit, w[:, k : k + 1], 0.0)
        chosen = chosen + jnp.where(hit, 1.0, 0.0)
    earlier = lax.broadcasted_iota(jnp.int32, (count, count), 0) > lax.broadcasted_iota(
        jnp.int32, (count, count), 1
    )
    rank = jnp.dot(earlier.astype(BF16), chosen.astype(BF16), preferred_element_type=F32)
    slots = EXPERTS * ROOM
    column = lax.broadcasted_iota(jnp.int32, (EXPERTS, slots), 1)
    owner = lax.broadcasted_iota(jnp.int32, (EXPERTS, slots), 0)
    inside = column - owner * ROOM
    spread = jnp.where((inside >= 0) & (inside < ROOM), 1.0, 0.0)
    slot = jnp.sum(jnp.where(spread > 0, inside.astype(F32), 0.0), axis=0, keepdims=True)
    spread_low = spread.astype(BF16)
    hits = jnp.dot(chosen.astype(BF16), spread_low, preferred_element_type=F32)
    ranks = jnp.dot(rank.astype(BF16), spread_low, preferred_element_type=F32)
    weights = jnp.dot(weight, spread, precision=lax.Precision.HIGHEST)
    placed = (hits > 0.5) & (ranks == slot)
    combine_ref[...] = jnp.where(placed, weights, 0.0)
    onehot = jnp.where(placed, 1.0, 0.0).astype(BF16)
    out_ref[...] = lax.dot_general(
        onehot, tokens_ref[...], CONTRACT_FIRST, preferred_element_type=F32
    ).astype(BF16)


def packing(tall, wide, by_row):
    row = lax.broadcasted_iota(jnp.int32, (tall, wide), 0)
    column = lax.broadcasted_iota(jnp.int32, (tall, wide), 1)
    tight, loose = (row, column) if by_row else (column, row)
    block = lax.shift_right_logical(tight * 3641, 16)
    return jnp.where(loose == tight + block * (ROOM - CAP), 1.0, 0.0).astype(BF16)


def products_kernel(place, own_ref, sibling_ref, gate_ref, up_ref, swapped_ref, out_ref):
    start = pl.multiple_of(place[1] * HALF, HALF)
    pack = packing(ROWS, EXPERTS * ROOM, True)
    own = jnp.dot(pack, own_ref[...], preferred_element_type=F32).astype(BF16)
    sibling = jnp.dot(pack, sibling_ref[...], preferred_element_type=F32).astype(BF16)
    parts = out_ref.shape[0]
    rows = ROWS // parts
    for i in range(parts):
        a, b = own[i * rows : (i + 1) * rows], sibling[i * rows : (i + 1) * rows]
        for j, mine in enumerate((gate_ref, up_ref)):
            out_ref[i, :, j * HALF : (j + 1) * HALF] = (
                jnp.dot(a, mine[:, pl.ds(start, HALF)], preferred_element_type=F32)
                + jnp.dot(b, swapped_ref[j], preferred_element_type=F32)
            ).astype(BF16)


def sum_kernel(place, parts_ref, wide_ref, low_ref):
    total = parts_ref[0].astype(F32)
    for i in range(1, parts_ref.shape[0]):
        total = total + parts_ref[i].astype(F32)
    wide_ref[...] = total
    low_ref[...] = total.astype(BF16)


def hidden_kernel(place, wide_ref, other_ref, out_ref):
    total = wide_ref[...] + other_ref[...].astype(F32)
    gate, up = total[:, :HALF], total[:, HALF:]
    hidden = (gate / (1.0 + jnp.exp(-gate)) * up).astype(BF16)
    for i in range(out_ref.shape[0]):
        out_ref[i] = hidden


def project_kernel(place, hidden_ref, down_ref, swapped_ref, own_ref, sibling_ref):
    start = pl.multiple_of(place[1] * HALF, HALF)
    parts = hidden_ref.shape[0]
    rows = ROWS // parts
    for i in range(parts):
        sl = slice(i * rows, (i + 1) * rows)
        h = hidden_ref[i]
        sibling_ref[sl] = jnp.dot(h, swapped_ref[...], preferred_element_type=F32).astype(BF16)
        own_ref[sl] = jnp.dot(h, down_ref[pl.ds(start, HALF), :], preferred_element_type=F32)


def finish_kernel(place, own_ref, other_ref, out_ref):
    result = (own_ref[...] + other_ref[...].astype(F32)).astype(BF16)
    unpack = packing(EXPERTS * ROOM, ROWS, False)
    out_ref[...] = jnp.dot(unpack, result, preferred_element_type=F32).astype(BF16)


def combine_kernel(place, combine_ref, back_ref, out_ref):
    c = combine_ref[...]
    back = back_ref[...]
    total = jnp.zeros(out_ref.shape, F32)
    for _ in range(3):
        part = c.astype(BF16)
        total = total + jnp.dot(part, back, preferred_element_type=F32)
        c = c - part.astype(F32)
    out_ref[...] = total.astype(BF16)


def body(
    queries,
    key_states,
    value_states,
    token_states,
    expert_ids,
    combine_weights,
    gate_weight,
    up_weight,
    down_weight,
):
    core, z_lo = lax.axis_index("c"), lax.axis_index("z")
    shard = (lax.axis_index("w") * lax.axis_size("x") + lax.axis_index("x")) * 2 + core
    place = jnp.stack([shard, core]).astype(jnp.int32)
    head = z_lo * HD
    kv = jnp.concatenate(
        [
            lax.dynamic_slice_in_dim(key_states, head, HD, 1),
            lax.dynamic_slice_in_dim(value_states, head, HD, 1),
        ],
        axis=1,
    )
    gate, up, down = gate_weight[0], up_weight[0], down_weight[0]
    width = token_states.shape[1]
    swap = lambda a: lax.ppermute(a, "c", [(0, 1), (1, 0)])

    kv_all = lax.all_gather(kv, ("w", "x", "c"), axis=0, tiled=True)

    slots = EXPERTS * ROOM
    outbound, combine_map = call(
        dispatch_kernel,
        (shape((slots, width)), shape((token_states.shape[0], slots), F32)),
        (place, expert_ids, combine_weights, token_states),
        flops=2 * slots * 64 * 400,
        moved=1 << 20,
        name="dispatch",
    )
    received = lax.all_to_all(
        outbound.reshape(EXPERTS, ROOM, width), ("z", "y"), 0, 0, tiled=True
    ).reshape(slots, width)
    other_half = (1 - core) * HALF
    swapped = swap(
        jnp.stack(
            [
                lax.dynamic_slice_in_dim(gate, other_half, HALF, 1),
                lax.dynamic_slice_in_dim(up, other_half, HALF, 1),
            ]
        )
    )
    swapped_down = swap(lax.dynamic_slice_in_dim(down, other_half, HALF, 0))
    sibling = swap(received)
    lanes = lax.axis_size("x")
    rows = ROWS // lanes
    products = call(
        products_kernel,
        shape((lanes, rows, FF)),
        (place, received, sibling, gate, up, swapped),
        flops=2 * ROWS * 2 * width * FF,
        moved=4 << 20,
        name="products",
    )
    parts = lax.all_to_all(products, "x", 0, 0, tiled=True)
    wide, low = call(
        sum_kernel,
        (shape((rows, FF), F32), shape((rows, FF))),
        (place, parts),
        flops=rows * FF * 4,
        moved=3 << 20,
        name="sum_parts",
    )
    other = lax.ppermute(low, "w", [(0, 1), (1, 0)])
    hidden = call(
        hidden_kernel,
        shape((lanes, rows, HALF)),
        (place, wide, other),
        flops=rows * FF * 4,
        moved=2 << 20,
        transcendentals=rows * HALF,
        name="hidden",
    )
    hidden_all = lax.all_to_all(hidden, "x", 0, 0, tiled=True)
    own_part, sibling_part = call(
        project_kernel,
        (shape((ROWS, width), F32), shape((ROWS, width))),
        (place, hidden_all, down, swapped_down),
        flops=2 * ROWS * HALF * 2 * width,
        moved=3 << 20,
        name="project",
    )
    finished = call(
        finish_kernel,
        shape((slots, width)),
        (place, own_part, swap(sibling_part)),
        flops=2 * ROWS * slots * width,
        moved=2 << 20,
        name="finish",
    )
    back = lax.all_to_all(finished.reshape(EXPERTS, ROOM, width), ("z", "y"), 0, 0, tiled=True)
    moe_output = call(
        combine_kernel,
        shape(token_states.shape),
        (place, combine_map, back.reshape(slots, width)),
        flops=6 * slots * width * 64,
        moved=1 << 20,
        name="combine",
    )
    context = attention(place, queries, kv_all)
    return (context, moe_output)


def solution(mesh):
    fine = Mesh(mesh.devices.reshape(2, 4, 2, 4, 8), ("w", "x", "c", "z", "y"))
    ctx, exp = ("w", "x", "c"), ("z", "y")
    in_specs = (
        P(ctx, exp),
        P(ctx, None),
        P(ctx, None),
        P(exp, ctx),
        P(exp, None),
        P(exp, None),
        P(exp, ctx, None),
        P(exp, ctx, None),
        P(exp, None, ctx),
    )
    out_specs = (P(ctx, exp), P(exp, ctx))
    return jax.shard_map(body, mesh=fine, in_specs=in_specs, out_specs=out_specs, check_vma=False)
```

```python
import jax
import jax.numpy as jnp
import numpy as np
from jax import lax
from jax.experimental import pallas as pl
from jax.experimental.pallas import tpu as pltpu
from jax.sharding import Mesh
from jax.sharding import PartitionSpec as P

FF = 1536
HEADS = 64
KVH = 4
HD = 128
TOPK = 8
EXPERTS = 32
CAP = 18
HALF_CAP = CAP // 2
GROUPS = 4
ROOM = 40
SLOTS = EXPERTS * ROOM
ROWS = EXPERTS * HALF_CAP
F32 = jnp.float32
BF16 = jnp.bfloat16
LOG2E = 1.4426950408889634
TILE = 256
CONTRACT_LAST = (((1,), (1,)), ((), ()))
CONTRACT_FIRST = (((0,), (0,)), ((), ()))
SMEM = pl.BlockSpec(memory_space=pltpu.SMEM)
VMEM = pl.BlockSpec(memory_space=pltpu.VMEM)


def call(
    kernel, outs, ins, flops, moved, limit=32, scratch=(), transcendentals=0, name=None, after=()
):
    count = len(ins)

    def run(*refs):
        kernel(*refs[:count], *refs[count + len(after) :])

    return pl.pallas_call(
        run,
        out_shape=outs,
        in_specs=[SMEM] + [VMEM] * (count - 1) + [pl.BlockSpec(memory_space=pl.ANY)] * len(after),
        out_specs=jax.tree.map(lambda _: VMEM, outs),
        scratch_shapes=scratch,
        compiler_params=pltpu.CompilerParams(vmem_limit_bytes=limit << 20),
        cost_estimate=pl.CostEstimate(
            flops=flops, bytes_accessed=moved, transcendentals=transcendentals
        ),
        name=name,
    )(*ins, *after)


def shape(dims, dtype=BF16):
    return jax.ShapeDtypeStruct(dims, dtype)


def spread_queries(q_ref, q2):
    rows, heads = q_ref.shape[0], q_ref.shape[1] // HD
    for h in range(heads):
        q = q_ref[:, h * HD : (h + 1) * HD].astype(F32) * (LOG2E * HD**-0.5)
        high = q.astype(BF16)
        q2[h * rows : (h + 1) * rows, :HD] = high
        q2[h * rows : (h + 1) * rows, HD:] = (q - high.astype(F32)).astype(BF16)


def key_block(kv_ref, i):
    k, v = kv_ref[i, :, :HD], kv_ref[i, :, HD:]
    return (
        jnp.concatenate([k, k], axis=1),
        jnp.concatenate([v, jnp.ones_like(v)], axis=1),
    )


def attend(q2, kk, v1, peak, acc, rows, diagonal):
    keys = kk.shape[0]
    for t in range(q2.shape[0] // TILE):
        sl = slice(t * TILE, (t + 1) * TILE)
        s = lax.dot_general(q2[sl, :], kk, CONTRACT_LAST, preferred_element_type=F32)
        if diagonal:
            query = (t * TILE) % rows + lax.broadcasted_iota(jnp.int32, (TILE, keys), 0)
            key = lax.broadcasted_iota(jnp.int32, (TILE, keys), 1)
            s = jnp.where(query >= key, s, -1e30)
        new = jnp.max(s, axis=1, keepdims=True)
        if not diagonal:
            old = peak[sl, :1]
            new = jnp.maximum(old, new)
        peak[sl, :] = jnp.broadcast_to(new, (TILE, HD))
        mixed = jnp.dot(jnp.exp2(s - new).astype(BF16), v1, preferred_element_type=F32)
        acc[sl, :] = mixed if diagonal else acc[sl, :] * jnp.exp2(old - new) + mixed


def attention_own_kernel(place, q_ref, kv_ref, sibling_ref, acc, peak, q2):
    rows = q_ref.shape[0]
    spread_queries(q_ref, q2)
    attend(q2, *key_block(kv_ref, 0), peak, acc, rows, True)

    def earlier(i, carry):
        attend(q2, *key_block(kv_ref, i), peak, acc, rows, False)
        return carry

    def earlier_sibling(i, carry):
        attend(q2, *key_block(sibling_ref, i), peak, acc, rows, False)
        return carry

    chip, core = place[0], place[1]
    lax.fori_loop(1, chip + 1, earlier, 0)
    lax.fori_loop(1 - core, chip + 1, earlier_sibling, 0)


def attention_far_kernel(place, q_ref, kv_ref, acc_in, peak_in, acc, peak, q2):
    spread_queries(q_ref, q2)
    acc[...] = acc_in[...]
    peak[...] = peak_in[...]

    def earlier(i, carry):
        attend(q2, *key_block(kv_ref, i), peak, acc, q_ref.shape[0], False)
        return carry

    lax.fori_loop(0, place[2] * kv_ref.shape[0], earlier, 0)


def attention_last_kernel(place, q_ref, kv_ref, acc_in, peak_in, o_ref, q2, acc, peak):
    rows, heads = q_ref.shape[0], q_ref.shape[1] // HD
    attention_far_kernel(place, q_ref, kv_ref, acc_in, peak_in, acc, peak, q2)
    for h in range(heads):
        a = acc[h * rows : (h + 1) * rows, :]
        o_ref[:, h * HD : (h + 1) * HD] = (a[:, :HD] / a[:, HD:]).astype(o_ref.dtype)


def attention(kernel, place, q, keys, state, last, name, after):
    stacked = q.shape[0] * q.shape[1] // HD
    results = (shape((stacked, 2 * HD), F32), shape((stacked, HD), F32))
    scratch = [pltpu.VMEM((stacked, 2 * HD), BF16)]
    if last:
        scratch = scratch + [pltpu.VMEM(r.shape, r.dtype) for r in results]
        results = shape(q.shape)
    count = sum(k.shape[0] * k.shape[1] for k in keys)
    return call(
        kernel,
        results,
        (place, q, *keys, *state),
        flops=4 * stacked * count * HD,
        moved=5 << 20,
        transcendentals=stacked * count,
        scratch=scratch,
        name=name,
        after=after,
    )


def places(ids_ref, core):
    count = ids_ref.shape[1]
    expert = lax.broadcasted_iota(jnp.int32, (EXPERTS, count), 0)
    chosen = jnp.zeros((EXPERTS, count), F32)
    for k in range(TOPK):
        chosen = chosen + jnp.where(ids_ref[k : k + 1, :] == expert, 1.0, 0.0)
    chosen = chosen.astype(BF16)
    earlier = lax.broadcasted_iota(jnp.int32, (count, count), 0) < lax.broadcasted_iota(
        jnp.int32, (count, count), 1
    )
    rank = jnp.dot(chosen, jnp.where(earlier, 1.0, 0.0).astype(BF16), preferred_element_type=F32)
    inside = lax.broadcasted_iota(jnp.int32, (SLOTS, EXPERTS), 0) - ROOM * lax.broadcasted_iota(
        jnp.int32, (SLOTS, EXPERTS), 1
    )
    own = (inside >= 0) & (inside < ROOM)
    spread = jnp.where(own, 1.0, 0.0).astype(BF16)
    row = jnp.sum(jnp.where(own, inside.astype(F32), 0.0), axis=1, keepdims=True)
    group = jnp.zeros_like(row)
    for g in range(1, GROUPS + 1):
        group = group + jnp.where(row >= g * HALF_CAP, 1.0, 0.0)
    wanted = row - group * HALF_CAP + (core * HALF_CAP).astype(F32)
    hits = jnp.dot(spread, chosen, preferred_element_type=F32)
    ranks = jnp.dot(spread, rank.astype(BF16), preferred_element_type=F32)
    placed = (hits > 0.5) & (ranks == wanted) & (group < GROUPS)
    return spread, placed, group


def dispatch_kernel(place, ids_ref, own_ref, sibling_ref, out_ref):
    core = place[1]
    _, placed, group = places(ids_ref, core)
    own, sibling = own_ref[...], sibling_ref[...]
    first, second = jnp.where(core == 0, own, sibling), jnp.where(core == 0, sibling, own)
    tokens = jnp.concatenate([first, second], axis=1)
    total = jnp.zeros(out_ref.shape, F32)
    for g in range(GROUPS):
        onehot = jnp.where(placed & (group == g), 1.0, 0.0).astype(BF16)
        total = total + jnp.dot(
            onehot, tokens[:, g * HD : (g + 1) * HD], preferred_element_type=F32
        )
    out_ref[...] = total.astype(BF16)


def combine_map_kernel(place, ids_ref, w_ref, out_ref):
    spread, placed, _ = places(ids_ref, place[1])
    expert = lax.broadcasted_iota(jnp.int32, (EXPERTS, ids_ref.shape[1]), 0)
    weight = jnp.zeros(expert.shape, F32)
    for k in range(TOPK):
        weight = weight + jnp.where(ids_ref[k : k + 1, :] == expert, w_ref[k : k + 1, :], 0.0)
    weights = jnp.dot(spread.astype(F32), weight, precision=lax.Precision.HIGHEST)
    out_ref[...] = jnp.where(placed, weights, 0.0)


def packing():
    row = np.arange(SLOTS)
    inside = row % ROOM
    tight = np.where(
        inside < GROUPS * HALF_CAP, row // ROOM * HALF_CAP + inside % HALF_CAP, -1
    )
    return jnp.asarray(np.arange(ROWS)[:, None] == tight[None, :], BF16)


def row_groups():
    row = lax.broadcasted_iota(jnp.int32, (SLOTS, 1), 0)
    inside = row - ROOM * lax.shift_right_logical(row * 1639, 16)
    group = jnp.zeros_like(row)
    for g in range(1, GROUPS + 1):
        group = group + jnp.where(inside >= g * HALF_CAP, 1, 0)
    return group


def widen(block):
    group = row_groups()
    return jnp.concatenate(
        [jnp.where(group == g, block, 0.0).astype(BF16) for g in range(GROUPS)], axis=1
    )


def products_kernel(
    place, pack_ref, rows_ref, gate_ref, up_ref, sibling_gate_ref, sibling_up_ref, out_ref
):
    rows = jnp.dot(pack_ref[...], widen(rows_ref[...]), preferred_element_type=F32)
    rows = rows.astype(BF16)
    half = rows.shape[1] // 2
    first, second = rows[:, :half], rows[:, half:]
    core = place[1]
    own, sibling = jnp.where(core == 0, first, second), jnp.where(core == 0, second, first)
    cols = out_ref.shape[2] // 2
    for i in range(out_ref.shape[0]):
        sl = slice(i * cols, (i + 1) * cols)
        for j, (mine, its) in enumerate(((gate_ref, sibling_gate_ref), (up_ref, sibling_up_ref))):
            out_ref[i, :, j * cols : (j + 1) * cols] = (
                jnp.dot(own, mine[:, sl], preferred_element_type=F32)
                + jnp.dot(sibling, its[:, sl], preferred_element_type=F32)
            ).astype(BF16)


def sum_kernel(place, parts_ref, wide_ref, low_ref):
    total = parts_ref[0].astype(F32)
    for i in range(1, parts_ref.shape[0]):
        total = total + parts_ref[i].astype(F32)
    wide_ref[...] = total
    low_ref[...] = total.astype(BF16)


def hidden_kernel(place, wide_ref, other_ref, out_ref):
    total = wide_ref[...] + other_ref[...].astype(F32)
    cols = total.shape[1] // 2
    gate, up = total[:, :cols], total[:, cols:]
    hidden = (gate / (1.0 + jnp.exp(-gate)) * up).astype(BF16)
    for i in range(out_ref.shape[0]):
        out_ref[i] = hidden


def project_kernel(place, pack_ref, hidden_ref, down_ref, swapped_ref, out_ref):
    hidden = jnp.concatenate([hidden_ref[i] for i in range(hidden_ref.shape[0])], axis=1)
    own = jnp.dot(hidden, down_ref[...], preferred_element_type=F32).astype(BF16)
    sibling = jnp.dot(hidden, swapped_ref[...], preferred_element_type=F32).astype(BF16)
    core = place[1]
    first, second = jnp.where(core == 0, own, sibling), jnp.where(core == 0, sibling, own)
    result = jnp.concatenate([first, second], axis=1)
    group = row_groups()
    wide = lax.dot_general(pack_ref[...], result, CONTRACT_FIRST, preferred_element_type=F32)
    total = jnp.zeros(out_ref.shape, F32)
    for g in range(GROUPS):
        total = jnp.where(group == g, wide[:, g * HD : (g + 1) * HD], total)
    out_ref[...] = total.astype(BF16)


def combine_kernel(place, combine_ref, back_ref, own_ref, sibling_ref):
    c, wide = combine_ref[...], widen(back_ref[...])
    total = jnp.zeros((c.shape[1], wide.shape[1]), F32)
    for _ in range(3):
        part = c.astype(BF16)
        total = total + lax.dot_general(part, wide, CONTRACT_FIRST, preferred_element_type=F32)
        c = c - part.astype(F32)
    half = total.shape[1] // 2
    core = place[1]
    own_ref[...] = jnp.where(core == 0, total[:, :half], total[:, half:])
    sibling_ref[...] = jnp.where(core == 0, total[:, half:], total[:, :half])


def add_kernel(place, own_ref, other_ref, out_ref):
    out_ref[...] = (own_ref[...] + other_ref[...]).astype(BF16)


def head_columns(heads, key_states, value_states, after):
    rows = key_states.shape[0]
    picks = [
        pl.BlockSpec((rows, HD), lambda i, at, n=n: (0, at[n])) for n in (0, 1) for _ in range(2)
    ]

    def run(place, key_ref, value_ref, other_key_ref, other_value_ref, *refs):
        out_ref, other_ref = refs[-2:]
        out_ref[:, :HD], out_ref[:, HD:] = key_ref[...], value_ref[...]
        other_ref[:, :HD], other_ref[:, HD:] = other_key_ref[...], other_value_ref[...]

    return pl.pallas_call(
        run,
        out_shape=[shape((rows, 2 * HD))] * 2,
        grid_spec=pltpu.PrefetchScalarGridSpec(
            num_scalar_prefetch=1,
            grid=(1,),
            in_specs=picks + [pl.BlockSpec(memory_space=pl.ANY)] * len(after),
            out_specs=[pl.BlockSpec((rows, 2 * HD), lambda i, at: (0, 0))] * 2,
        ),
        cost_estimate=pl.CostEstimate(flops=0, bytes_accessed=0, transcendentals=0),
        name="head_columns",
    )(
        jnp.stack(heads).astype(jnp.int32),
        key_states,
        value_states,
        key_states,
        value_states,
        *after,
    )


def stack_kernel(place, *refs):
    for i, ref in enumerate(refs[:-1]):
        refs[-1][i] = ref[...]


def stack(place, parts, after, name):
    return call(
        stack_kernel,
        shape((len(parts), *parts[0].shape)),
        (place, *parts),
        flops=0,
        moved=0,
        name=name,
        after=after,
    )


def body(
    queries,
    key_states,
    value_states,
    token_states,
    expert_ids,
    combine_weights,
    gate_weight,
    up_weight,
    down_weight,
):
    core, z_lo = lax.axis_index("c"), lax.axis_index("z")
    half = lax.axis_index("w")
    place = jnp.stack([lax.axis_index("x"), core, half]).astype(jnp.int32)
    swap = lambda a: lax.ppermute(a, "c", [(0, 1), (1, 0)])
    gate, up, down = gate_weight[0], up_weight[0], down_weight[0]
    count, width = token_states.shape
    ids = expert_ids.T
    block = (EXPERTS, ROOM, HD)
    pack = packing()

    outbound = call(
        dispatch_kernel,
        shape((SLOTS, HD)),
        (place, ids, token_states, swap(token_states)),
        flops=2 * SLOTS * 64 * 600,
        moved=1 << 20,
        name="dispatch",
    )
    received = lax.all_to_all(outbound.reshape(block), ("z", "y"), 0, 0, tiled=True)

    z_count, lanes = lax.axis_size("z"), lax.axis_size("x")
    kv, kv_near = head_columns(
        [z_lo, z_count - 1 - z_lo], key_states, value_states, (outbound,)
    )
    kv_far = lax.ppermute(
        kv_near, ("w", "z"), [(z, 2 * z_count - 1 - z) for z in range(z_count)]
    )
    near = [kv] + [
        lax.ppermute(kv, "x", [(x, x + k) for x in range(lanes - k)]) for k in range(1, lanes)
    ]
    far = [kv_far] + [
        lax.ppermute(
            kv_far, ("w", "x"), [(lanes + x, lanes + (x + k) % lanes) for x in range(lanes)]
        )
        for k in range(1, lanes)
    ]
    cols = 2 * FF // lanes
    products = call(
        products_kernel,
        shape((lanes, ROWS, cols)),
        (place, pack, received.reshape(SLOTS, HD), gate, up, swap(gate), swap(up)),
        flops=2 * ROWS * 4 * width * FF,
        moved=5 << 20,
        name="products",
    )
    parts = lax.all_to_all(products, "x", 0, 0, tiled=True)
    near = stack(place, near, (products,), "stack_near")
    acc, peak = attention(
        attention_own_kernel,
        place,
        queries,
        (near, swap(near)),
        (),
        False,
        "attention_near",
        (products,),
    )
    wide, low = call(
        sum_kernel,
        (shape((ROWS, cols), F32), shape((ROWS, cols))),
        (place, parts),
        flops=ROWS * cols * 4,
        moved=3 << 20,
        name="sum_parts",
        after=(acc, kv_far),
    )
    other = lax.ppermute(low, "w", [(0, 1), (1, 0)])
    combine_map = call(
        combine_map_kernel,
        shape((SLOTS, count), F32),
        (place, ids, combine_weights.T),
        flops=2 * SLOTS * 64 * 600,
        moved=1 << 20,
        name="combine_map",
        after=(low,),
    )
    hidden = call(
        hidden_kernel,
        shape((lanes, ROWS, cols // 2)),
        (place, wide, other),
        flops=ROWS * cols * 4,
        moved=2 << 20,
        transcendentals=ROWS * cols // 2,
        name="hidden",
    )
    hidden_all = lax.all_to_all(hidden, "x", 0, 0, tiled=True)
    far = stack(place, far, (hidden, combine_map), "stack_far")
    state = attention(
        attention_far_kernel,
        place,
        queries,
        (far,),
        (acc, peak),
        False,
        "attention_far",
        (hidden,),
    )
    finished = call(
        project_kernel,
        shape((SLOTS, HD)),
        (place, pack, hidden_all, down, swap(down)),
        flops=2 * ROWS * FF * 2 * width,
        moved=3 << 20,
        name="project",
        after=state,
    )
    back = lax.all_to_all(finished.reshape(block), ("z", "y"), 0, 0, tiled=True)
    context = attention(
        attention_last_kernel,
        place,
        queries,
        (swap(far),),
        state,
        True,
        "attention_last",
        (finished,),
    )
    own_sum, sibling_sum = call(
        combine_kernel,
        (shape((count, width), F32), shape((count, width), F32)),
        (place, combine_map, back.reshape(SLOTS, HD)),
        flops=6 * SLOTS * 2 * width * 64,
        moved=1 << 20,
        name="combine",
        after=(context,),
    )
    moe_output = call(
        add_kernel,
        shape((count, width)),
        (place, own_sum, swap(sibling_sum)),
        flops=count * width,
        moved=200 << 10,
        name="add_cores",
    )
    return (context, moe_output)


def solution(mesh):
    fine = Mesh(mesh.devices.reshape(2, 4, 2, 4, 8), ("w", "x", "c", "z", "y"))
    ctx, exp = ("w", "x", "c"), ("z", "y")
    in_specs = (
        P(ctx, exp),
        P(ctx, None),
        P(ctx, None),
        P(exp, ctx),
        P(exp, None),
        P(exp, None),
        P(exp, ctx, None),
        P(exp, ctx, None),
        P(exp, None, ctx),
    )
    out_specs = (P(ctx, exp), P(exp, ctx))
    return jax.shard_map(body, mesh=fine, in_specs=in_specs, out_specs=out_specs, check_vma=False)
```

```python
import jax
import jax.numpy as jnp
from jax import lax
from jax.experimental import pallas as pl
from jax.experimental.pallas import tpu as pltpu
from jax.sharding import Mesh
from jax.sharding import PartitionSpec as P

FF = 1536
HEADS = 64
KVH = 4
HD = 128
TOPK = 8
EXPERTS = 32
CAP = 18
HALF_CAP = CAP // 2
GROUPS = 4
ROOM = 40
SLOTS = EXPERTS * ROOM
ROWS = EXPERTS * HALF_CAP
F32 = jnp.float32
BF16 = jnp.bfloat16
LOG2E = 1.4426950408889634
TILE = 256
CONTRACT_LAST = (((1,), (1,)), ((), ()))
CONTRACT_FIRST = (((0,), (0,)), ((), ()))
VMEM = pl.BlockSpec(memory_space=pltpu.VMEM)
ANY = pl.BlockSpec(memory_space=pl.ANY)


def call(
    kernel, outs, ins, flops, moved, scratch=(), transcendentals=0, name=None, after=(),
    fetched=(), stored=(), bare=False,
):
    first = len(ins) + len(after)
    outs = [*outs, shape((8, HD), F32)]
    last = first + len(outs) - 1
    buffers = [] if bare else [ins[i] for i in fetched] + [outs[i] for i in stored]
    copies = len(buffers)

    def run(*refs):
        own = refs[last + 1 + copies :]
        if copies:
            *own, sems = own
            reads, writes = refs[: len(ins)], refs[first:last]
            near = refs[last + 1 : last + 1 + copies]
            into = dict(zip(fetched, near))
            out_of = dict(zip(stored, near[len(fetched) :]))
            moves = [
                pltpu.make_async_copy(reads[i], buffer, sems.at[k])
                for k, (i, buffer) in enumerate(into.items())
            ]
            for move in moves:
                move.start()
            for move in moves:
                move.wait()
            kernel(
                *[into.get(i, ref) for i, ref in enumerate(reads)],
                *[out_of.get(i, ref) for i, ref in enumerate(writes)],
                *own,
            )
            moves = [
                pltpu.make_async_copy(buffer, writes[i], sems.at[len(fetched) + k])
                for k, (i, buffer) in enumerate(out_of.items())
            ]
            for move in moves:
                move.start()
            for move in moves:
                move.wait()
        else:
            kernel(*refs[: len(ins)], *refs[first:last], *own)
        refs[last][...] = jnp.zeros(refs[last].shape, F32)

    return pl.pallas_call(
        run,
        out_shape=outs,
        in_specs=[ANY if i in fetched else VMEM for i in range(first)],
        out_specs=[ANY if i in stored else VMEM for i in range(len(outs))],
        scratch_shapes=[
            *[pltpu.VMEM(b.shape, b.dtype) for b in buffers],
            *scratch,
            *([pltpu.SemaphoreType.DMA((copies,))] if copies else []),
        ],
        compiler_params=pltpu.CompilerParams(vmem_limit_bytes=(60 if copies else 32) << 20),
        cost_estimate=pl.CostEstimate(
            flops=flops, bytes_accessed=moved, transcendentals=transcendentals
        ),
        name=name,
    )(*ins, *after)


def shape(dims, dtype=BF16):
    return jax.ShapeDtypeStruct(dims, dtype)


def spread_queries(q_ref, q2):
    rows, heads = q_ref.shape[0], q_ref.shape[1] // HD
    for h in range(heads):
        q = q_ref[:, h * HD : (h + 1) * HD].astype(F32) * (LOG2E * HD**-0.5)
        high = q.astype(BF16)
        q2[h * rows : (h + 1) * rows, :HD] = high
        q2[h * rows : (h + 1) * rows, HD:] = (q - high.astype(F32)).astype(BF16)


def key_block(kv_ref, i):
    k, v = kv_ref[i, :, :HD], kv_ref[i, :, HD:]
    return (
        jnp.concatenate([k, k], axis=1),
        jnp.concatenate([v, jnp.ones_like(v)], axis=1),
    )


def attend(q2, blocks, peak, acc, rows, diagonal=False):
    tiles = [slice(at, at + TILE) for at in range(0, q2.shape[0], TILE)]

    def scores_of(sl):
        out = []
        for kk, _ in blocks:
            s = lax.dot_general(q2[sl, :], kk, CONTRACT_LAST, preferred_element_type=F32)
            if diagonal:
                query = sl.start % rows + lax.broadcasted_iota(jnp.int32, s.shape, 0)
                key = lax.broadcasted_iota(jnp.int32, s.shape, 1)
                s = jnp.where(query >= key, s, -1e30)
            out.append(s)
        return out

    ahead = scores_of(tiles[0])
    for t, sl in enumerate(tiles):
        scores = ahead
        if t + 1 < len(tiles):
            ahead = scores_of(tiles[t + 1])
        highest = scores[0]
        for s in scores[1:]:
            highest = jnp.maximum(highest, s)
        new = jnp.max(highest, axis=1, keepdims=True)
        if not diagonal:
            old = peak[sl, :1]
            new = jnp.maximum(old, new)
        mixed = 0.0 if diagonal else acc[sl, :] * jnp.exp2(old - new)
        for s, (_, v1) in zip(scores, blocks):
            p = jnp.exp2(s - new).astype(BF16)
            mixed = mixed + jnp.dot(p, v1, preferred_element_type=F32)
        acc[sl, :] = mixed
        peak[sl, :] = jnp.broadcast_to(new, (TILE, HD))


def attention_near_kernel(q_ref, kv_ref, sibling_ref, acc, peak, q2):
    rows = q_ref.shape[0]
    spread_queries(q_ref, q2)
    attend(q2, [key_block(kv_ref, 0)], peak, acc, rows, True)

    def beside(i, carry):
        attend(q2, [key_block(sibling_ref, 0)], peak, acc, rows)
        return carry

    def earlier(i, carry):
        attend(q2, [key_block(kv_ref, i), key_block(sibling_ref, i)], peak, acc, rows)
        return carry

    chip, core = lax.axis_index("x"), lax.axis_index("c")
    lax.fori_loop(0, core, beside, 0)
    lax.fori_loop(1, chip + 1, earlier, 0)


def attention_far_kernel(q, kv, sibling, acc, peak, o_ref, q2):
    rows, heads = q.shape[0], q.shape[1] // HD
    spread_queries(q, q2)

    def earlier(i, carry):
        blocks = [key_block(ref, 2 * i + j) for j in (0, 1) for ref in (kv, sibling)]
        attend(q2, blocks, peak, acc, rows)
        return carry

    lax.fori_loop(0, lax.axis_index("w") * (kv.shape[0] // 2), earlier, 0)
    for h in range(heads):
        a = acc[h * rows : (h + 1) * rows, :]
        o_ref[:, h * HD : (h + 1) * HD] = (a[:, :HD] / a[:, HD:]).astype(o_ref.dtype)


def attention(kernel, outs, ins, fetched, name, after):
    stacked, keys = ins[0].shape[0] * ins[0].shape[1] // HD, 8 * ins[0].shape[0]
    return call(
        kernel,
        outs,
        ins,
        flops=4 * stacked * keys * HD,
        moved=5 << 20,
        transcendentals=stacked * keys,
        scratch=[pltpu.VMEM((stacked, 2 * HD), BF16)],
        name=name,
        after=after,
        fetched=fetched,
    )


def places(ids_ref, core):
    count = ids_ref.shape[1]
    expert = lax.broadcasted_iota(jnp.int32, (EXPERTS, count), 0)
    chosen = jnp.zeros((EXPERTS, count), F32)
    for k in range(TOPK):
        chosen = chosen + jnp.where(ids_ref[k : k + 1, :] == expert, 1.0, 0.0)
    chosen = chosen.astype(BF16)
    earlier = lax.broadcasted_iota(jnp.int32, (count, count), 0) < lax.broadcasted_iota(
        jnp.int32, (count, count), 1
    )
    rank = jnp.dot(chosen, jnp.where(earlier, 1.0, 0.0).astype(BF16), preferred_element_type=F32)
    inside = lax.broadcasted_iota(jnp.int32, (SLOTS, EXPERTS), 0) - ROOM * lax.broadcasted_iota(
        jnp.int32, (SLOTS, EXPERTS), 1
    )
    own = (inside >= 0) & (inside < ROOM)
    spread = jnp.where(own, 1.0, 0.0).astype(BF16)
    row = jnp.sum(jnp.where(own, inside.astype(F32), 0.0), axis=1, keepdims=True)
    group = jnp.zeros_like(row)
    for g in range(1, GROUPS + 1):
        group = group + jnp.where(row >= g * HALF_CAP, 1.0, 0.0)
    wanted = row - group * HALF_CAP + (core * HALF_CAP).astype(F32)
    hits = jnp.dot(spread, chosen, preferred_element_type=F32)
    ranks = jnp.dot(spread, rank.astype(BF16), preferred_element_type=F32)
    placed = (hits > 0.5) & (ranks == wanted) & (group < GROUPS)
    return spread, placed, group


def dispatch_kernel(ids_ref, own_ref, sibling_ref, out_ref):
    core = lax.axis_index("c")
    _, placed, group = places(ids_ref, core)
    own, sibling = own_ref[...], sibling_ref[...]
    first, second = jnp.where(core == 0, own, sibling), jnp.where(core == 0, sibling, own)
    tokens = jnp.concatenate([first, second], axis=1)
    total = jnp.zeros(out_ref.shape, F32)
    for g in range(GROUPS):
        onehot = jnp.where(placed & (group == g), 1.0, 0.0).astype(BF16)
        total = total + jnp.dot(
            onehot, tokens[:, g * HD : (g + 1) * HD], preferred_element_type=F32
        )
    out_ref[...] = total.astype(BF16)


def combine_map_kernel(ids_ref, w_ref, out_ref):
    spread, placed, _ = places(ids_ref, lax.axis_index("c"))
    expert = lax.broadcasted_iota(jnp.int32, (EXPERTS, ids_ref.shape[1]), 0)
    weight = jnp.zeros(expert.shape, F32)
    for k in range(TOPK):
        weight = weight + jnp.where(ids_ref[k : k + 1, :] == expert, w_ref[k : k + 1, :], 0.0)
    weights = jnp.dot(spread.astype(F32), weight, precision=lax.Precision.HIGHEST)
    out_ref[...] = jnp.where(placed, weights, 0.0)


def block_rows(dims, axis):
    row = lax.broadcasted_iota(jnp.int32, dims, axis)
    expert = lax.shift_right_logical(row * 1639, 16)
    inside = row - ROOM * expert
    group = jnp.zeros_like(row)
    for g in range(1, GROUPS + 1):
        group = group + jnp.where(inside >= g * HALF_CAP, 1, 0)
    tight = expert * HALF_CAP + inside - HALF_CAP * group
    return jnp.where(group < GROUPS, tight, -1), group


def widen(block):
    _, group = block_rows((SLOTS, 1), 0)
    return jnp.concatenate(
        [jnp.where(group == g, block, 0.0).astype(BF16) for g in range(GROUPS)], axis=1
    )


def products_kernel(
    rows_ref, gate_ref, up_ref, sibling_gate_ref, sibling_up_ref, out_ref
):
    tight, _ = block_rows((1, SLOTS), 1)
    pack = jnp.where(tight == lax.broadcasted_iota(jnp.int32, (ROWS, SLOTS), 0), 1.0, 0.0)
    rows = jnp.dot(pack.astype(BF16), widen(rows_ref[...]), preferred_element_type=F32)
    rows = rows.astype(BF16)
    half = rows.shape[1] // 2
    first, second = rows[:, :half], rows[:, half:]
    core = lax.axis_index("c")
    own, sibling = jnp.where(core == 0, first, second), jnp.where(core == 0, second, first)
    cols = out_ref.shape[2] // 2
    for i in range(out_ref.shape[0]):
        sl = slice(i * cols, (i + 1) * cols)
        for j, (mine, its) in enumerate(((gate_ref, sibling_gate_ref), (up_ref, sibling_up_ref))):
            out_ref[i, :, j * cols : (j + 1) * cols] = (
                jnp.dot(own, mine[:, sl], preferred_element_type=F32)
                + jnp.dot(sibling, its[:, sl], preferred_element_type=F32)
            ).astype(BF16)


def sum_kernel(parts_ref, wide_ref, low_ref):
    total = parts_ref[0].astype(F32)
    for i in range(1, parts_ref.shape[0]):
        total = total + parts_ref[i].astype(F32)
    wide_ref[...] = total
    low_ref[...] = total.astype(BF16)


def hidden_kernel(wide_ref, other_ref, out_ref):
    total = wide_ref[...] + other_ref[...].astype(F32)
    cols = total.shape[1] // 2
    gate, up = total[:, :cols], total[:, cols:]
    out_ref[...] = (gate / (1.0 + jnp.exp(-gate)) * up).astype(BF16)


def project_kernel(hidden_ref, down_ref, swapped_ref, out_ref):
    hidden = jnp.concatenate([hidden_ref[i] for i in range(hidden_ref.shape[0])], axis=1)
    own = jnp.dot(hidden, down_ref[...], preferred_element_type=F32).astype(BF16)
    sibling = jnp.dot(hidden, swapped_ref[...], preferred_element_type=F32).astype(BF16)
    core = lax.axis_index("c")
    first, second = jnp.where(core == 0, own, sibling), jnp.where(core == 0, sibling, own)
    result = jnp.concatenate([first, second], axis=1)
    tight, group = block_rows((SLOTS, 1), 0)
    unpack = jnp.where(tight == lax.broadcasted_iota(jnp.int32, (SLOTS, ROWS), 1), 1.0, 0.0)
    wide = jnp.dot(unpack.astype(BF16), result, preferred_element_type=F32)
    total = jnp.zeros(out_ref.shape, F32)
    for g in range(GROUPS):
        total = jnp.where(group == g, wide[:, g * HD : (g + 1) * HD], total)
    out_ref[...] = total.astype(BF16)


def combine_kernel(combine_ref, back_ref, own_ref, sibling_ref):
    c, wide = combine_ref[...], widen(back_ref[...])
    total = jnp.zeros((c.shape[1], wide.shape[1]), F32)
    for _ in range(3):
        part = c.astype(BF16)
        total = total + lax.dot_general(part, wide, CONTRACT_FIRST, preferred_element_type=F32)
        c = c - part.astype(F32)
    half = total.shape[1] // 2
    core = lax.axis_index("c")
    own_ref[...] = jnp.where(core == 0, total[:, :half], total[:, half:])
    sibling_ref[...] = jnp.where(core == 0, total[:, half:], total[:, :half])


def add_kernel(own_ref, other_ref, out_ref):
    out_ref[...] = (own_ref[...] + other_ref[...]).astype(BF16)


def head_columns_kernel(key_ref, value_ref, kv_ref, near_ref, sems):
    z = lax.axis_index("z")
    copies = []
    for i, (out, head) in enumerate(((kv_ref, z), (near_ref, KVH - 1 - z))):
        columns = pl.ds(pl.multiple_of(head * HD, HD), HD)
        for j, source in enumerate((key_ref, value_ref)):
            copies.append(
                pltpu.make_async_copy(
                    source.at[:, columns], out.at[:, j * HD : (j + 1) * HD], sems.at[2 * i + j]
                )
            )
    for copy in copies:
        copy.start()
    for copy in copies:
        copy.wait()


def stack_kernel(*refs):
    for i, ref in enumerate(refs[:-1]):
        refs[-1][i] = ref[...]


def stack(parts, after, name):
    return call(
        stack_kernel,
        [shape((len(parts), *parts[0].shape))],
        parts,
        flops=0,
        moved=0,
        name=name,
        after=after,
    )[0]


def body(
    queries,
    key_states,
    value_states,
    token_states,
    expert_ids,
    combine_weights,
    gate_weight,
    up_weight,
    down_weight,
):
    swap = lambda a: lax.ppermute(a, "c", [(0, 1), (1, 0)])
    gate, up, down = gate_weight[0], up_weight[0], down_weight[0]
    count, width = token_states.shape
    ids = expert_ids.T
    block = (EXPERTS, ROOM, HD)

    outbound, sent = call(
        dispatch_kernel,
        [shape((SLOTS, HD))],
        (ids, token_states, swap(token_states)),
        flops=2 * SLOTS * 64 * 600,
        moved=1 << 20,
        name="dispatch",
    )
    received = lax.all_to_all(outbound.reshape(block), ("z", "y"), 0, 0, tiled=True)

    z_count, lanes = lax.axis_size("z"), lax.axis_size("x")
    kv, kv_near, _ = call(
        head_columns_kernel,
        [shape((key_states.shape[0], 2 * HD))] * 2,
        (key_states, value_states),
        flops=0,
        moved=0,
        scratch=[pltpu.SemaphoreType.DMA((4,))],
        name="head_columns",
        after=(sent,),
        fetched=(0, 1),
        bare=True,
    )
    kv_far = lax.ppermute(
        kv_near, ("w", "z"), [(z, 2 * z_count - 1 - z) for z in range(z_count)]
    )
    near = [kv] + [
        lax.ppermute(kv, "x", [(x, x + k) for x in range(lanes - k)]) for k in range(1, lanes)
    ]
    far = [kv_far] + [
        lax.ppermute(
            kv_far, ("w", "x"), [(lanes + x, lanes + (x + k) % lanes) for x in range(lanes)]
        )
        for k in range(1, lanes)
    ]
    cols = 2 * FF // lanes
    products, multiplied = call(
        products_kernel,
        [shape((lanes, ROWS, cols))],
        (received.reshape(SLOTS, HD), gate, up, swap(gate), swap(up)),
        flops=2 * ROWS * 4 * width * FF,
        moved=5 << 20,
        name="products",
    )
    parts = lax.all_to_all(products, "x", 0, 0, tiled=True)
    near = stack(near, (multiplied,), "stack_near")
    stacked = queries.shape[0] * queries.shape[1] // HD
    spread = shape((stacked, 2 * HD))
    running = [shape((stacked, 2 * HD), F32), shape((stacked, HD), F32)]
    stacked = queries.shape[0] * queries.shape[1] // HD
    *state, seen = attention(
        attention_near_kernel,
        [shape((stacked, 2 * HD), F32), shape((stacked, HD), F32)],
        (queries, near, swap(near)),
        (),
        "attention_near",
        (multiplied,),
    )
    wide, low, summed = call(
        sum_kernel,
        [shape((ROWS, cols), F32), shape((ROWS, cols))],
        (parts,),
        flops=ROWS * cols * 4,
        moved=3 << 20,
        name="sum_parts",
        after=(seen, kv_far),
    )
    other = lax.ppermute(low, "w", [(0, 1), (1, 0)])
    combine_map, mapped = call(
        combine_map_kernel,
        [shape((SLOTS, count), F32)],
        (ids, combine_weights.T),
        flops=0,
        moved=0,
        name="combine_map",
        after=(summed,),
    )
    hidden, ready = call(
        hidden_kernel,
        [shape((ROWS, cols // 2))],
        (wide, other),
        flops=ROWS * cols * 4,
        moved=2 << 20,
        transcendentals=ROWS * cols // 2,
        name="hidden",
        after=(mapped,),
    )
    hidden_all = lax.all_gather(hidden, "x", axis=0)
    far = stack(far, (ready,), "stack_far")
    finished, projected = call(
        project_kernel,
        [shape((SLOTS, HD))],
        (hidden_all, down, swap(down)),
        flops=2 * ROWS * FF * 2 * width,
        moved=3 << 20,
        name="project",
    )
    back = lax.all_to_all(finished.reshape(block), ("z", "y"), 0, 0, tiled=True)
    context, seen = attention(
        attention_far_kernel,
        [shape(queries.shape)],
        (queries, far, swap(far), *state),
        range(5),
        "attention_far",
        (projected,),
    )
    own_sum, sibling_sum, _ = call(
        combine_kernel,
        [shape((count, width), F32), shape((count, width), F32)],
        (combine_map, back.reshape(SLOTS, HD)),
        flops=6 * SLOTS * 2 * width * 64,
        moved=1 << 20,
        name="combine",
        after=(seen,),
    )
    moe_output, _ = call(
        add_kernel,
        [shape((count, width))],
        (own_sum, swap(sibling_sum)),
        flops=count * width,
        moved=200 << 10,
        name="add_cores",
    )
    return (context, moe_output)


def solution(mesh):
    fine = Mesh(mesh.devices.reshape(2, 4, 2, 4, 8), ("w", "x", "c", "z", "y"))
    ctx, exp = ("w", "x", "c"), ("z", "y")
    in_specs = (
        P(ctx, exp),
        P(ctx, None),
        P(ctx, None),
        P(exp, ctx),
        P(exp, None),
        P(exp, None),
        P(exp, ctx, None),
        P(exp, ctx, None),
        P(exp, None, ctx),
    )
    out_specs = (P(ctx, exp), P(exp, ctx))
    return jax.shard_map(body, mesh=fine, in_specs=in_specs, out_specs=out_specs, check_vma=False)
```

```python
import jax
import jax.numpy as jnp
from jax import lax
from jax.experimental import pallas as pl
from jax.experimental.pallas import tpu as pltpu
from jax.sharding import Mesh
from jax.sharding import PartitionSpec as P

FF = 1536
HEADS = 64
KVH = 4
HD = 128
TOPK = 8
EXPERTS = 32
CAP = 18
HALF_CAP = CAP // 2
GROUPS = 4
ROOM = 40
SLOTS = EXPERTS * ROOM
ROWS = EXPERTS * HALF_CAP
F32 = jnp.float32
BF16 = jnp.bfloat16
LOG2E = 1.4426950408889634
TILE = 256
CONTRACT_LAST = (((1,), (1,)), ((), ()))
CONTRACT_FIRST = (((0,), (0,)), ((), ()))
VMEM = pl.BlockSpec(memory_space=pltpu.VMEM)
ANY = pl.BlockSpec(memory_space=pl.ANY)


def call(
    kernel, outs, ins, flops, moved, scratch=(), transcendentals=0, name=None, after=(),
    fetched=(), stored=(), bare=False,
):
    first = len(ins) + len(after)
    outs = [*outs, shape((8, HD), F32)]
    last = first + len(outs) - 1
    buffers = [] if bare else [ins[i] for i in fetched] + [outs[i] for i in stored]
    copies = len(buffers)

    def run(*refs):
        own = refs[last + 1 + copies :]
        if copies:
            *own, sems = own
            reads, writes = refs[: len(ins)], refs[first:last]
            near = refs[last + 1 : last + 1 + copies]
            into = dict(zip(fetched, near))
            out_of = dict(zip(stored, near[len(fetched) :]))
            moves = [
                pltpu.make_async_copy(reads[i], buffer, sems.at[k])
                for k, (i, buffer) in enumerate(into.items())
            ]
            for move in moves:
                move.start()
            for move in moves:
                move.wait()
            kernel(
                *[into.get(i, ref) for i, ref in enumerate(reads)],
                *[out_of.get(i, ref) for i, ref in enumerate(writes)],
                *own,
            )
            moves = [
                pltpu.make_async_copy(buffer, writes[i], sems.at[len(fetched) + k])
                for k, (i, buffer) in enumerate(out_of.items())
            ]
            for move in moves:
                move.start()
            for move in moves:
                move.wait()
        else:
            kernel(*refs[: len(ins)], *refs[first:last], *own)
        refs[last][...] = jnp.zeros(refs[last].shape, F32)

    return pl.pallas_call(
        run,
        out_shape=outs,
        in_specs=[ANY if i in fetched else VMEM for i in range(first)],
        out_specs=[ANY if i in stored else VMEM for i in range(len(outs))],
        scratch_shapes=[
            *[pltpu.VMEM(b.shape, b.dtype) for b in buffers],
            *scratch,
            *([pltpu.SemaphoreType.DMA((copies,))] if copies else []),
        ],
        compiler_params=pltpu.CompilerParams(vmem_limit_bytes=(60 if fetched else 32) << 20),
        cost_estimate=pl.CostEstimate(
            flops=flops, bytes_accessed=moved, transcendentals=transcendentals
        ),
        name=name,
    )(*ins, *after)


def shape(dims, dtype=BF16):
    return jax.ShapeDtypeStruct(dims, dtype)


def spread_queries(q_ref, q2):
    rows, heads = q_ref.shape[0], q_ref.shape[1] // HD
    for h in range(heads):
        q = q_ref[:, h * HD : (h + 1) * HD].astype(F32) * (LOG2E * HD**-0.5)
        high = q.astype(BF16)
        q2[h * rows : (h + 1) * rows, :HD] = high
        q2[h * rows : (h + 1) * rows, HD:] = (q - high.astype(F32)).astype(BF16)


def key_block(kv_ref, i):
    k, v = kv_ref[i, :, :HD], kv_ref[i, :, HD:]
    return (
        jnp.concatenate([k, k], axis=1),
        jnp.concatenate([v, jnp.ones_like(v)], axis=1),
    )


def attend(q2, blocks, peak, acc, rows, diagonal=False):
    tiles = [slice(at, at + TILE) for at in range(0, q2.shape[0], TILE)]

    def scores_of(sl):
        out = []
        for kk, _ in blocks:
            s = lax.dot_general(q2[sl, :], kk, CONTRACT_LAST, preferred_element_type=F32)
            if diagonal:
                query = sl.start % rows + lax.broadcasted_iota(jnp.int32, s.shape, 0)
                key = lax.broadcasted_iota(jnp.int32, s.shape, 1)
                s = jnp.where(query >= key, s, -1e30)
            out.append(s)
        return out

    ahead = scores_of(tiles[0])
    for t, sl in enumerate(tiles):
        scores = ahead
        if t + 1 < len(tiles):
            ahead = scores_of(tiles[t + 1])
        highest = scores[0]
        for s in scores[1:]:
            highest = jnp.maximum(highest, s)
        new = jnp.max(highest, axis=1, keepdims=True)
        if not diagonal:
            old = peak[sl, :1]
            new = jnp.maximum(old, new)
        mixed = 0.0 if diagonal else acc[sl, :] * jnp.exp2(old - new)
        for s, (_, v1) in zip(scores, blocks):
            p = jnp.exp2(s - new).astype(BF16)
            mixed = mixed + jnp.dot(p, v1, preferred_element_type=F32)
        acc[sl, :] = mixed
        peak[sl, :] = jnp.broadcast_to(new, (TILE, HD))


def attention_near_kernel(q_ref, kv_ref, sibling_ref, acc, peak, q2):
    rows = q_ref.shape[0]
    spread_queries(q_ref, q2)
    attend(q2, [key_block(kv_ref, 0)], peak, acc, rows, True)

    def beside(i, carry):
        attend(q2, [key_block(sibling_ref, 0)], peak, acc, rows)
        return carry

    def earlier(i, carry):
        attend(q2, [key_block(kv_ref, i), key_block(sibling_ref, i)], peak, acc, rows)
        return carry

    chip, core = lax.axis_index("x"), lax.axis_index("c")
    lax.fori_loop(0, core, beside, 0)
    lax.fori_loop(1, chip + 1, earlier, 0)


def attention_far_kernel(q, kv, sibling, acc, peak, o_ref, q2):
    rows, heads = q.shape[0], q.shape[1] // HD
    spread_queries(q, q2)

    def earlier(i, carry):
        blocks = [key_block(ref, 2 * i + j) for j in (0, 1) for ref in (kv, sibling)]
        attend(q2, blocks, peak, acc, rows)
        return carry

    lax.fori_loop(0, lax.axis_index("w") * (kv.shape[0] // 2), earlier, 0)
    for h in range(heads):
        a = acc[h * rows : (h + 1) * rows, :]
        o_ref[:, h * HD : (h + 1) * HD] = (a[:, :HD] / a[:, HD:]).astype(o_ref.dtype)


def attention(kernel, outs, ins, fetched, name, after):
    stacked, keys = ins[0].shape[0] * ins[0].shape[1] // HD, 8 * ins[0].shape[0]
    return call(
        kernel,
        outs,
        ins,
        flops=4 * stacked * keys * HD,
        moved=5 << 20,
        transcendentals=stacked * keys,
        scratch=[pltpu.VMEM((stacked, 2 * HD), BF16)],
        name=name,
        after=after,
        fetched=fetched,
    )


def places(ids_ref, core):
    count = ids_ref.shape[1]
    expert = lax.broadcasted_iota(jnp.int32, (EXPERTS, count), 0)
    chosen = jnp.zeros((EXPERTS, count), F32)
    for k in range(TOPK):
        chosen = chosen + jnp.where(ids_ref[k : k + 1, :] == expert, 1.0, 0.0)
    chosen = chosen.astype(BF16)
    earlier = lax.broadcasted_iota(jnp.int32, (count, count), 0) < lax.broadcasted_iota(
        jnp.int32, (count, count), 1
    )
    rank = jnp.dot(chosen, jnp.where(earlier, 1.0, 0.0).astype(BF16), preferred_element_type=F32)
    inside = lax.broadcasted_iota(jnp.int32, (SLOTS, EXPERTS), 0) - ROOM * lax.broadcasted_iota(
        jnp.int32, (SLOTS, EXPERTS), 1
    )
    own = (inside >= 0) & (inside < ROOM)
    spread = jnp.where(own, 1.0, 0.0).astype(BF16)
    row = jnp.sum(jnp.where(own, inside.astype(F32), 0.0), axis=1, keepdims=True)
    group = jnp.zeros_like(row)
    for g in range(1, GROUPS + 1):
        group = group + jnp.where(row >= g * HALF_CAP, 1.0, 0.0)
    wanted = row - group * HALF_CAP + (core * HALF_CAP).astype(F32)
    hits = jnp.dot(spread, chosen, preferred_element_type=F32)
    ranks = jnp.dot(spread, rank.astype(BF16), preferred_element_type=F32)
    placed = (hits > 0.5) & (ranks == wanted) & (group < GROUPS)
    return spread, placed, group


def dispatch_kernel(ids_ref, own_ref, sibling_ref, out_ref):
    core = lax.axis_index("c")
    _, placed, group = places(ids_ref, core)
    own, sibling = own_ref[...], sibling_ref[...]
    first, second = jnp.where(core == 0, own, sibling), jnp.where(core == 0, sibling, own)
    tokens = jnp.concatenate([first, second], axis=1)
    total = jnp.zeros(out_ref.shape, F32)
    for g in range(GROUPS):
        onehot = jnp.where(placed & (group == g), 1.0, 0.0).astype(BF16)
        total = total + jnp.dot(
            onehot, tokens[:, g * HD : (g + 1) * HD], preferred_element_type=F32
        )
    out_ref[...] = total.astype(BF16)


def combine_map_kernel(ids_ref, w_ref, out_ref):
    spread, placed, _ = places(ids_ref, lax.axis_index("c"))
    expert = lax.broadcasted_iota(jnp.int32, (EXPERTS, ids_ref.shape[1]), 0)
    weight = jnp.zeros(expert.shape, F32)
    for k in range(TOPK):
        weight = weight + jnp.where(ids_ref[k : k + 1, :] == expert, w_ref[k : k + 1, :], 0.0)
    weights = jnp.dot(spread.astype(F32), weight, precision=lax.Precision.HIGHEST)
    out_ref[...] = jnp.where(placed, weights, 0.0)


def block_rows(dims, axis):
    row = lax.broadcasted_iota(jnp.int32, dims, axis)
    expert = lax.shift_right_logical(row * 1639, 16)
    inside = row - ROOM * expert
    group = jnp.zeros_like(row)
    for g in range(1, GROUPS + 1):
        group = group + jnp.where(inside >= g * HALF_CAP, 1, 0)
    tight = expert * HALF_CAP + inside - HALF_CAP * group
    return jnp.where(group < GROUPS, tight, -1), group


def widen(block):
    _, group = block_rows((SLOTS, 1), 0)
    return jnp.concatenate(
        [jnp.where(group == g, block, 0.0).astype(BF16) for g in range(GROUPS)], axis=1
    )


def products_kernel(rows_ref, own_ref, sibling_ref, out_ref):
    tight, _ = block_rows((1, SLOTS), 1)
    pack = jnp.where(tight == lax.broadcasted_iota(jnp.int32, (ROWS, SLOTS), 0), 1.0, 0.0)
    rows = jnp.dot(pack.astype(BF16), widen(rows_ref[...]), preferred_element_type=F32)
    rows = rows.astype(BF16)
    half = rows.shape[1] // 2
    first, second = rows[:, :half], rows[:, half:]
    core = lax.axis_index("c")
    own, sibling = jnp.where(core == 0, first, second), jnp.where(core == 0, second, first)
    cols = out_ref.shape[2] // 2
    for i in range(out_ref.shape[0]):
        sl = slice(i * cols, (i + 1) * cols)
        for j in range(2):
            out_ref[i, :, j * cols : (j + 1) * cols] = (
                jnp.dot(own, own_ref[j, :, sl], preferred_element_type=F32)
                + jnp.dot(sibling, sibling_ref[j, :, sl], preferred_element_type=F32)
            ).astype(BF16)


def sum_kernel(parts_ref, wide_ref, low_ref):
    total = parts_ref[0].astype(F32)
    for i in range(1, parts_ref.shape[0]):
        total = total + parts_ref[i].astype(F32)
    wide_ref[...] = total
    low_ref[...] = total.astype(BF16)


def hidden_kernel(wide_ref, other_ref, out_ref):
    total = wide_ref[...] + other_ref[...].astype(F32)
    cols = total.shape[1] // 2
    gate, up = total[:, :cols], total[:, cols:]
    out_ref[...] = (gate / (1.0 + jnp.exp(-gate)) * up).astype(BF16)


def project_kernel(hidden_ref, down_ref, swapped_ref, out_ref):
    hidden = jnp.concatenate([hidden_ref[i] for i in range(hidden_ref.shape[0])], axis=1)
    own = jnp.dot(hidden, down_ref[...], preferred_element_type=F32).astype(BF16)
    sibling = jnp.dot(hidden, swapped_ref[...], preferred_element_type=F32).astype(BF16)
    core = lax.axis_index("c")
    first, second = jnp.where(core == 0, own, sibling), jnp.where(core == 0, sibling, own)
    result = jnp.concatenate([first, second], axis=1)
    tight, group = block_rows((SLOTS, 1), 0)
    unpack = jnp.where(tight == lax.broadcasted_iota(jnp.int32, (SLOTS, ROWS), 1), 1.0, 0.0)
    wide = jnp.dot(unpack.astype(BF16), result, preferred_element_type=F32)
    total = jnp.zeros(out_ref.shape, F32)
    for g in range(GROUPS):
        total = jnp.where(group == g, wide[:, g * HD : (g + 1) * HD], total)
    out_ref[...] = total.astype(BF16)


def combine_kernel(combine_ref, back_ref, own_ref, sibling_ref):
    c, wide = combine_ref[...], widen(back_ref[...])
    total = jnp.zeros((c.shape[1], wide.shape[1]), F32)
    for _ in range(3):
        part = c.astype(BF16)
        total = total + lax.dot_general(part, wide, CONTRACT_FIRST, preferred_element_type=F32)
        c = c - part.astype(F32)
    half = total.shape[1] // 2
    core = lax.axis_index("c")
    own_ref[...] = jnp.where(core == 0, total[:, :half], total[:, half:])
    sibling_ref[...] = jnp.where(core == 0, total[:, half:], total[:, :half])


def add_kernel(own_ref, other_ref, out_ref):
    out_ref[...] = (own_ref[...] + other_ref[...]).astype(BF16)


def head_columns_kernel(key_ref, value_ref, kv_ref, near_ref, sems):
    z = lax.axis_index("z")
    copies = []
    for i, (out, head) in enumerate(((kv_ref, z), (near_ref, KVH - 1 - z))):
        columns = pl.ds(pl.multiple_of(head * HD, HD), HD)
        for j, source in enumerate((key_ref, value_ref)):
            copies.append(
                pltpu.make_async_copy(
                    source.at[:, columns], out.at[:, j * HD : (j + 1) * HD], sems.at[2 * i + j]
                )
            )
    for copy in copies:
        copy.start()
    for copy in copies:
        copy.wait()


def stack_kernel(*refs):
    for i, ref in enumerate(refs[:-1]):
        refs[-1][i] = ref[...]


def stack(parts, after, name):
    return call(
        stack_kernel,
        [shape((len(parts), *parts[0].shape))],
        parts,
        flops=0,
        moved=0,
        name=name,
        after=after,
    )


def body(
    queries,
    key_states,
    value_states,
    token_states,
    expert_ids,
    combine_weights,
    gate_weight,
    up_weight,
    down_weight,
):
    swap = lambda a: lax.ppermute(a, "c", [(0, 1), (1, 0)])
    gate, up, down = gate_weight[0], up_weight[0], down_weight[0]
    count, width = token_states.shape
    ids = expert_ids.T
    block = (EXPERTS, ROOM, HD)

    outbound, _ = call(
        dispatch_kernel,
        [shape((SLOTS, HD))],
        (ids, token_states, swap(token_states)),
        flops=2 * SLOTS * 64 * 600,
        moved=1 << 20,
        name="dispatch",
    )
    received = lax.all_to_all(outbound.reshape(block), ("z", "y"), 0, 0, tiled=True)

    z_count, lanes = lax.axis_size("z"), lax.axis_size("x")
    kv, kv_near, _ = call(
        head_columns_kernel,
        [shape((key_states.shape[0], 2 * HD))] * 2,
        (key_states, value_states),
        flops=0,
        moved=0,
        scratch=[pltpu.SemaphoreType.DMA((4,))],
        name="head_columns",
        fetched=(0, 1),
        bare=True,
    )
    kv_far = lax.ppermute(
        kv_near, ("w", "z"), [(z, 2 * z_count - 1 - z) for z in range(z_count)]
    )
    near = [kv] + [
        lax.ppermute(kv, "x", [(x, x + k) for x in range(lanes - k)]) for k in range(1, lanes)
    ]
    far = [kv_far] + [
        lax.ppermute(
            kv_far, ("w", "x"), [(lanes + x, lanes + (x + k) % lanes) for x in range(lanes)]
        )
        for k in range(1, lanes)
    ]
    cols = 2 * FF // lanes
    gate_up, _ = stack((gate, up), (), "pair_weights")
    products, multiplied = call(
        products_kernel,
        [shape((lanes, ROWS, cols))],
        (received.reshape(SLOTS, HD), gate_up, swap(gate_up)),
        flops=2 * ROWS * 4 * width * FF,
        moved=5 << 20,
        name="products",
    )
    parts = lax.all_to_all(products, "x", 0, 0, tiled=True)
    near, _ = stack(near, (multiplied,), "stack_near")
    stacked = queries.shape[0] * queries.shape[1] // HD
    spread = shape((stacked, 2 * HD))
    running = [shape((stacked, 2 * HD), F32), shape((stacked, HD), F32)]
    stacked = queries.shape[0] * queries.shape[1] // HD
    *state, seen = attention(
        attention_near_kernel,
        [shape((stacked, 2 * HD), F32), shape((stacked, HD), F32)],
        (queries, near, swap(near)),
        (),
        "attention_near",
        (multiplied,),
    )
    wide, low, summed = call(
        sum_kernel,
        [shape((ROWS, cols), F32), shape((ROWS, cols))],
        (parts,),
        flops=ROWS * cols * 4,
        moved=3 << 20,
        name="sum_parts",
        after=(seen, kv_far),
    )
    other = lax.ppermute(low, "w", [(0, 1), (1, 0)])
    combine_map, mapped = call(
        combine_map_kernel,
        [shape((SLOTS, count), F32)],
        (ids, combine_weights.T),
        flops=0,
        moved=0,
        name="combine_map",
        after=(summed,),
    )
    hidden, ready = call(
        hidden_kernel,
        [shape((ROWS, cols // 2))],
        (wide, other),
        flops=ROWS * cols * 4,
        moved=2 << 20,
        transcendentals=ROWS * cols // 2,
        name="hidden",
        after=(mapped,),
    )
    hidden_all = lax.all_gather(hidden, "x", axis=0)
    far, _ = stack(far, (ready,), "stack_far")
    finished, projected = call(
        project_kernel,
        [shape((SLOTS, HD))],
        (hidden_all, down, swap(down)),
        flops=2 * ROWS * FF * 2 * width,
        moved=3 << 20,
        name="project",
    )
    back = lax.all_to_all(finished.reshape(block), ("z", "y"), 0, 0, tiled=True)
    context, seen = attention(
        attention_far_kernel,
        [shape(queries.shape)],
        (queries, far, swap(far), *state),
        range(5),
        "attention_far",
        (projected,),
    )
    own_sum, sibling_sum, _ = call(
        combine_kernel,
        [shape((count, width), F32), shape((count, width), F32)],
        (combine_map, back.reshape(SLOTS, HD)),
        flops=6 * SLOTS * 2 * width * 64,
        moved=1 << 20,
        name="combine",
        after=(seen,),
    )
    moe_output, _ = call(
        add_kernel,
        [shape((count, width))],
        (own_sum, swap(sibling_sum)),
        flops=count * width,
        moved=200 << 10,
        name="add_cores",
    )
    return (context, moe_output)


def solution(mesh):
    fine = Mesh(mesh.devices.reshape(2, 4, 2, 4, 8), ("w", "x", "c", "z", "y"))
    ctx, exp = ("w", "x", "c"), ("z", "y")
    in_specs = (
        P(ctx, exp),
        P(ctx, None),
        P(ctx, None),
        P(exp, ctx),
        P(exp, None),
        P(exp, None),
        P(exp, ctx, None),
        P(exp, ctx, None),
        P(exp, None, ctx),
    )
    out_specs = (P(ctx, exp), P(exp, ctx))
    return jax.shard_map(body, mesh=fine, in_specs=in_specs, out_specs=out_specs, check_vma=False)
```

```python
import jax
import jax.numpy as jnp
from jax import lax
from jax.experimental import pallas as pl
from jax.experimental.pallas import tpu as pltpu
from jax.sharding import Mesh
from jax.sharding import PartitionSpec as P

FF = 1536
HEADS = 64
KVH = 4
HD = 128
TOPK = 8
EXPERTS = 32
CAP = 18
HALF_CAP = CAP // 2
GROUPS = 4
ROOM = 40
SLOTS = EXPERTS * ROOM
ROWS = EXPERTS * HALF_CAP
F32 = jnp.float32
BF16 = jnp.bfloat16
LOG2E = 1.4426950408889634
TILE = 256
CONTRACT_LAST = (((1,), (1,)), ((), ()))
CONTRACT_FIRST = (((0,), (0,)), ((), ()))
VMEM = pl.BlockSpec(memory_space=pltpu.VMEM)
ANY = pl.BlockSpec(memory_space=pl.ANY)


def call(
    kernel, outs, ins, flops, moved, scratch=(), transcendentals=0, name=None, after=(),
    fetched=(), stored=(), bare=False,
):
    first = len(ins) + len(after)
    outs = [*outs, shape((8, HD), F32)]
    last = first + len(outs) - 1
    buffers = [] if bare else [ins[i] for i in fetched] + [outs[i] for i in stored]
    copies = len(buffers)

    def run(*refs):
        own = refs[last + 1 + copies :]
        if copies:
            *own, sems = own
            reads, writes = refs[: len(ins)], refs[first:last]
            near = refs[last + 1 : last + 1 + copies]
            into = dict(zip(fetched, near))
            out_of = dict(zip(stored, near[len(fetched) :]))
            moves = [
                pltpu.make_async_copy(reads[i], buffer, sems.at[k])
                for k, (i, buffer) in enumerate(into.items())
            ]
            for move in moves:
                move.start()
            for move in moves:
                move.wait()
            kernel(
                *[into.get(i, ref) for i, ref in enumerate(reads)],
                *[out_of.get(i, ref) for i, ref in enumerate(writes)],
                *own,
            )
            moves = [
                pltpu.make_async_copy(buffer, writes[i], sems.at[len(fetched) + k])
                for k, (i, buffer) in enumerate(out_of.items())
            ]
            for move in moves:
                move.start()
            for move in moves:
                move.wait()
        else:
            kernel(*refs[: len(ins)], *refs[first:last], *own)
        refs[last][...] = jnp.zeros(refs[last].shape, F32)

    return pl.pallas_call(
        run,
        out_shape=outs,
        in_specs=[ANY if i in fetched else VMEM for i in range(first)],
        out_specs=[ANY if i in stored else VMEM for i in range(len(outs))],
        scratch_shapes=[
            *[pltpu.VMEM(b.shape, b.dtype) for b in buffers],
            *scratch,
            *([pltpu.SemaphoreType.DMA((copies,))] if copies else []),
        ],
        compiler_params=pltpu.CompilerParams(vmem_limit_bytes=(60 if fetched else 32) << 20),
        cost_estimate=pl.CostEstimate(
            flops=flops, bytes_accessed=moved, transcendentals=transcendentals
        ),
        name=name,
    )(*ins, *after)


def shape(dims, dtype=BF16):
    return jax.ShapeDtypeStruct(dims, dtype)


def spread_queries(q_ref, q2):
    rows, heads = q_ref.shape[0], q_ref.shape[1] // HD
    for h in range(heads):
        q = q_ref[:, h * HD : (h + 1) * HD].astype(F32) * (LOG2E * HD**-0.5)
        high = q.astype(BF16)
        q2[h * rows : (h + 1) * rows, :HD] = high
        q2[h * rows : (h + 1) * rows, HD:] = (q - high.astype(F32)).astype(BF16)


def key_block(kv_ref, i):
    k, v = kv_ref[i, :, :HD], kv_ref[i, :, HD:]
    return (
        jnp.concatenate([k, k], axis=1),
        jnp.concatenate([v, jnp.ones_like(v)], axis=1),
    )


def attend(q2, blocks, peak, acc, rows, diagonal=False):
    tiles = [slice(at, at + TILE) for at in range(0, q2.shape[0], TILE)]

    def scores_of(sl):
        out = []
        for kk, _ in blocks:
            s = lax.dot_general(q2[sl, :], kk, CONTRACT_LAST, preferred_element_type=F32)
            if diagonal:
                query = sl.start % rows + lax.broadcasted_iota(jnp.int32, s.shape, 0)
                key = lax.broadcasted_iota(jnp.int32, s.shape, 1)
                s = jnp.where(query >= key, s, -1e30)
            out.append(s)
        return out

    ahead = scores_of(tiles[0])
    for t, sl in enumerate(tiles):
        scores = ahead
        if t + 1 < len(tiles):
            ahead = scores_of(tiles[t + 1])
        highest = scores[0]
        for s in scores[1:]:
            highest = jnp.maximum(highest, s)
        new = jnp.max(highest, axis=1, keepdims=True)
        if not diagonal:
            old = peak[sl, :1]
            new = jnp.maximum(old, new)
        mixed = 0.0 if diagonal else acc[sl, :] * jnp.exp2(old - new)
        for s, (_, v1) in zip(scores, blocks):
            p = jnp.exp2(s - new).astype(BF16)
            mixed = mixed + jnp.dot(p, v1, preferred_element_type=F32)
        acc[sl, :] = mixed
        peak[sl, :] = jnp.broadcast_to(new, (TILE, HD))


def attention_near_kernel(q_ref, kv_ref, sibling_ref, acc, peak, q2):
    rows = q_ref.shape[0]
    spread_queries(q_ref, q2)
    attend(q2, [key_block(kv_ref, 0)], peak, acc, rows, True)

    def beside(i, carry):
        attend(q2, [key_block(sibling_ref, 0)], peak, acc, rows)
        return carry

    def earlier(i, carry):
        attend(q2, [key_block(kv_ref, i), key_block(sibling_ref, i)], peak, acc, rows)
        return carry

    chip, core = lax.axis_index("x"), lax.axis_index("c")
    lax.fori_loop(0, core, beside, 0)
    lax.fori_loop(1, chip + 1, earlier, 0)


def attention_far_kernel(q, kv, sibling, acc, peak, o_ref, q2):
    rows, heads = q.shape[0], q.shape[1] // HD
    spread_queries(q, q2)

    def earlier(i, carry):
        blocks = [key_block(ref, 2 * i + j) for j in (0, 1) for ref in (kv, sibling)]
        attend(q2, blocks, peak, acc, rows)
        return carry

    lax.fori_loop(0, lax.axis_index("w") * (kv.shape[0] // 2), earlier, 0)
    for h in range(heads):
        a = acc[h * rows : (h + 1) * rows, :]
        o_ref[:, h * HD : (h + 1) * HD] = (a[:, :HD] / a[:, HD:]).astype(o_ref.dtype)


def attention(kernel, outs, ins, fetched, name, after):
    stacked, keys = ins[0].shape[0] * ins[0].shape[1] // HD, 8 * ins[0].shape[0]
    return call(
        kernel,
        outs,
        ins,
        flops=4 * stacked * keys * HD,
        moved=5 << 20,
        transcendentals=stacked * keys,
        scratch=[pltpu.VMEM((stacked, 2 * HD), BF16)],
        name=name,
        after=after,
        fetched=fetched,
    )


def places(ids_ref, core):
    count = ids_ref.shape[1]
    expert = lax.broadcasted_iota(jnp.int32, (EXPERTS, count), 0)
    chosen = jnp.zeros((EXPERTS, count), F32)
    for k in range(TOPK):
        chosen = chosen + jnp.where(ids_ref[k : k + 1, :] == expert, 1.0, 0.0)
    chosen = chosen.astype(BF16)
    earlier = lax.broadcasted_iota(jnp.int32, (count, count), 0) < lax.broadcasted_iota(
        jnp.int32, (count, count), 1
    )
    rank = jnp.dot(chosen, jnp.where(earlier, 1.0, 0.0).astype(BF16), preferred_element_type=F32)
    inside = lax.broadcasted_iota(jnp.int32, (SLOTS, EXPERTS), 0) - ROOM * lax.broadcasted_iota(
        jnp.int32, (SLOTS, EXPERTS), 1
    )
    own = (inside >= 0) & (inside < ROOM)
    spread = jnp.where(own, 1.0, 0.0).astype(BF16)
    row = jnp.sum(jnp.where(own, inside.astype(F32), 0.0), axis=1, keepdims=True)
    group = jnp.zeros_like(row)
    for g in range(1, GROUPS + 1):
        group = group + jnp.where(row >= g * HALF_CAP, 1.0, 0.0)
    wanted = row - group * HALF_CAP + (core * HALF_CAP).astype(F32)
    hits = jnp.dot(spread, chosen, preferred_element_type=F32)
    ranks = jnp.dot(spread, rank.astype(BF16), preferred_element_type=F32)
    placed = (hits > 0.5) & (ranks == wanted) & (group < GROUPS)
    return spread, placed, group


def dispatch_kernel(ids_ref, own_ref, sibling_ref, out_ref):
    core = lax.axis_index("c")
    _, placed, group = places(ids_ref, core)
    own, sibling = own_ref[...], sibling_ref[...]
    first, second = jnp.where(core == 0, own, sibling), jnp.where(core == 0, sibling, own)
    tokens = jnp.concatenate([first, second], axis=1)
    total = jnp.zeros(out_ref.shape, F32)
    for g in range(GROUPS):
        onehot = jnp.where(placed & (group == g), 1.0, 0.0).astype(BF16)
        total = total + jnp.dot(
            onehot, tokens[:, g * HD : (g + 1) * HD], preferred_element_type=F32
        )
    out_ref[...] = total.astype(BF16)


def combine_map_kernel(ids_ref, w_ref, out_ref):
    spread, placed, _ = places(ids_ref, lax.axis_index("c"))
    expert = lax.broadcasted_iota(jnp.int32, (EXPERTS, ids_ref.shape[1]), 0)
    weight = jnp.zeros(expert.shape, F32)
    for k in range(TOPK):
        weight = weight + jnp.where(ids_ref[k : k + 1, :] == expert, w_ref[k : k + 1, :], 0.0)
    weights = jnp.dot(spread.astype(F32), weight, precision=lax.Precision.HIGHEST)
    out_ref[...] = jnp.where(placed, weights, 0.0)


def block_rows(dims, axis):
    row = lax.broadcasted_iota(jnp.int32, dims, axis)
    expert = lax.shift_right_logical(row * 1639, 16)
    inside = row - ROOM * expert
    group = jnp.zeros_like(row)
    for g in range(1, GROUPS + 1):
        group = group + jnp.where(inside >= g * HALF_CAP, 1, 0)
    tight = expert * HALF_CAP + inside - HALF_CAP * group
    return jnp.where(group < GROUPS, tight, -1), group


def widen(block):
    _, group = block_rows((SLOTS, 1), 0)
    return jnp.concatenate(
        [jnp.where(group == g, block, 0.0).astype(BF16) for g in range(GROUPS)], axis=1
    )


def products_kernel(rows_ref, gate_ref, up_ref, sibling_gate_ref, sibling_up_ref, out_ref):
    tight, _ = block_rows((1, SLOTS), 1)
    pack = jnp.where(tight == lax.broadcasted_iota(jnp.int32, (ROWS, SLOTS), 0), 1.0, 0.0)
    rows = jnp.dot(pack.astype(BF16), widen(rows_ref[...]), preferred_element_type=F32)
    rows = rows.astype(BF16)
    half = rows.shape[1] // 2
    first, second = rows[:, :half], rows[:, half:]
    core = lax.axis_index("c")
    own, sibling = jnp.where(core == 0, first, second), jnp.where(core == 0, second, first)
    cols = out_ref.shape[2] // 2
    for i in range(out_ref.shape[0]):
        sl = slice(i * cols, (i + 1) * cols)
        for j, (mine, its) in enumerate(((gate_ref, sibling_gate_ref), (up_ref, sibling_up_ref))):
            out_ref[i, :, j * cols : (j + 1) * cols] = (
                jnp.dot(own, mine[:, sl], preferred_element_type=F32)
                + jnp.dot(sibling, its[:, sl], preferred_element_type=F32)
            ).astype(BF16)


def sum_kernel(parts_ref, wide_ref, low_ref):
    total = parts_ref[0].astype(F32)
    for i in range(1, parts_ref.shape[0]):
        total = total + parts_ref[i].astype(F32)
    wide_ref[...] = total
    low_ref[...] = total.astype(BF16)


def hidden_kernel(wide_ref, other_ref, out_ref):
    total = wide_ref[...] + other_ref[...].astype(F32)
    cols = total.shape[1] // 2
    gate, up = total[:, :cols], total[:, cols:]
    out_ref[...] = (gate / (1.0 + jnp.exp(-gate)) * up).astype(BF16)


def project_kernel(hidden_ref, down_ref, swapped_ref, out_ref):
    hidden = jnp.concatenate([hidden_ref[i] for i in range(hidden_ref.shape[0])], axis=1)
    own = jnp.dot(hidden, down_ref[...], preferred_element_type=F32).astype(BF16)
    sibling = jnp.dot(hidden, swapped_ref[...], preferred_element_type=F32).astype(BF16)
    core = lax.axis_index("c")
    first, second = jnp.where(core == 0, own, sibling), jnp.where(core == 0, sibling, own)
    result = jnp.concatenate([first, second], axis=1)
    tight, group = block_rows((SLOTS, 1), 0)
    unpack = jnp.where(tight == lax.broadcasted_iota(jnp.int32, (SLOTS, ROWS), 1), 1.0, 0.0)
    wide = jnp.dot(unpack.astype(BF16), result, preferred_element_type=F32)
    total = jnp.zeros(out_ref.shape, F32)
    for g in range(GROUPS):
        total = jnp.where(group == g, wide[:, g * HD : (g + 1) * HD], total)
    out_ref[...] = total.astype(BF16)


def combine_kernel(combine_ref, back_ref, own_ref, sibling_ref):
    c, wide = combine_ref[...], widen(back_ref[...])
    total = jnp.zeros((c.shape[1], wide.shape[1]), F32)
    for _ in range(3):
        part = c.astype(BF16)
        total = total + lax.dot_general(part, wide, CONTRACT_FIRST, preferred_element_type=F32)
        c = c - part.astype(F32)
    half = total.shape[1] // 2
    core = lax.axis_index("c")
    own_ref[...] = jnp.where(core == 0, total[:, :half], total[:, half:])
    sibling_ref[...] = jnp.where(core == 0, total[:, half:], total[:, :half])


def add_kernel(own_ref, other_ref, out_ref):
    out_ref[...] = (own_ref[...] + other_ref[...]).astype(BF16)


def head_columns_kernel(key_ref, value_ref, kv_ref, near_ref, sems):
    z = lax.axis_index("z")
    copies = []
    for i, (out, head) in enumerate(((kv_ref, z), (near_ref, KVH - 1 - z))):
        columns = pl.ds(pl.multiple_of(head * HD, HD), HD)
        for j, source in enumerate((key_ref, value_ref)):
            copies.append(
                pltpu.make_async_copy(
                    source.at[:, columns], out.at[:, j * HD : (j + 1) * HD], sems.at[2 * i + j]
                )
            )
    for copy in copies:
        copy.start()
    for copy in copies:
        copy.wait()


def stack_kernel(*refs):
    for i, ref in enumerate(refs[:-1]):
        refs[-1][i] = ref[...]


def stack(parts, after, name):
    return call(
        stack_kernel,
        [shape((len(parts), *parts[0].shape))],
        parts,
        flops=0,
        moved=0,
        name=name,
        after=after,
    )


def body(
    queries,
    key_states,
    value_states,
    token_states,
    expert_ids,
    combine_weights,
    gate_weight,
    up_weight,
    down_weight,
):
    swap = lambda a: lax.ppermute(a, "c", [(0, 1), (1, 0)])
    gate, up, down = gate_weight[0], up_weight[0], down_weight[0]
    count, width = token_states.shape
    ids = expert_ids.T
    block = (EXPERTS, ROOM, HD)

    outbound, _ = call(
        dispatch_kernel,
        [shape((SLOTS, HD))],
        (ids, token_states, swap(token_states)),
        flops=2 * SLOTS * 64 * 600,
        moved=1 << 20,
        name="dispatch",
    )
    received = lax.all_to_all(outbound.reshape(block), ("z", "y"), 0, 0, tiled=True)

    z_count, lanes = lax.axis_size("z"), lax.axis_size("x")
    kv, kv_near, _ = call(
        head_columns_kernel,
        [shape((key_states.shape[0], 2 * HD))] * 2,
        (key_states, value_states),
        flops=0,
        moved=0,
        scratch=[pltpu.SemaphoreType.DMA((4,))],
        name="head_columns",
        fetched=(0, 1),
        bare=True,
    )
    kv_far = lax.ppermute(
        kv_near, ("w", "z"), [(z, 2 * z_count - 1 - z) for z in range(z_count)]
    )
    near = [kv] + [
        lax.ppermute(kv, "x", [(x, x + k) for x in range(lanes - k)]) for k in range(1, lanes)
    ]
    far = [kv_far] + [
        lax.ppermute(
            kv_far, ("w", "x"), [(lanes + x, lanes + (x + k) % lanes) for x in range(lanes)]
        )
        for k in range(1, lanes)
    ]
    cols = 2 * FF // lanes
    products, multiplied = call(
        products_kernel,
        [shape((lanes, ROWS, cols))],
        (received.reshape(SLOTS, HD), gate, up, swap(gate), swap(up)),
        flops=2 * ROWS * 4 * width * FF,
        moved=5 << 20,
        name="products",
    )
    parts = lax.all_to_all(products, "x", 0, 0, tiled=True)
    near, _ = stack(near, (multiplied,), "stack_near")
    stacked = queries.shape[0] * queries.shape[1] // HD
    spread = shape((stacked, 2 * HD))
    running = [shape((stacked, 2 * HD), F32), shape((stacked, HD), F32)]
    stacked = queries.shape[0] * queries.shape[1] // HD
    *state, seen = attention(
        attention_near_kernel,
        [shape((stacked, 2 * HD), F32), shape((stacked, HD), F32)],
        (queries, near, swap(near)),
        (),
        "attention_near",
        (multiplied,),
    )
    wide, low, summed = call(
        sum_kernel,
        [shape((ROWS, cols), F32), shape((ROWS, cols))],
        (parts,),
        flops=ROWS * cols * 4,
        moved=3 << 20,
        name="sum_parts",
        after=(seen, kv_far),
    )
    other = lax.ppermute(low, "w", [(0, 1), (1, 0)])
    combine_map, mapped = call(
        combine_map_kernel,
        [shape((SLOTS, count), F32)],
        (ids, combine_weights.T),
        flops=0,
        moved=0,
        name="combine_map",
        after=(summed,),
    )
    hidden, ready = call(
        hidden_kernel,
        [shape((ROWS, cols // 2))],
        (wide, other),
        flops=ROWS * cols * 4,
        moved=2 << 20,
        transcendentals=ROWS * cols // 2,
        name="hidden",
        after=(mapped,),
    )
    hidden_all = lax.all_gather(hidden, "x", axis=0)
    far, _ = stack(far, (ready,), "stack_far")
    finished, projected = call(
        project_kernel,
        [shape((SLOTS, HD))],
        (hidden_all, down, swap(down)),
        flops=2 * ROWS * FF * 2 * width,
        moved=3 << 20,
        name="project",
    )
    back = lax.all_to_all(finished.reshape(block), ("z", "y"), 0, 0, tiled=True)
    context, seen = attention(
        attention_far_kernel,
        [shape(queries.shape)],
        (queries, far, swap(far), *state),
        range(5),
        "attention_far",
        (projected,),
    )
    own_sum, sibling_sum, _ = call(
        combine_kernel,
        [shape((count, width), F32), shape((count, width), F32)],
        (combine_map, back.reshape(SLOTS, HD)),
        flops=6 * SLOTS * 2 * width * 64,
        moved=1 << 20,
        name="combine",
        after=(seen,),
    )
    moe_output, _ = call(
        add_kernel,
        [shape((count, width))],
        (own_sum, swap(sibling_sum)),
        flops=count * width,
        moved=200 << 10,
        name="add_cores",
    )
    return (context, moe_output)


def solution(mesh):
    fine = Mesh(mesh.devices.reshape(2, 4, 2, 4, 8), ("w", "x", "c", "z", "y"))
    ctx, exp = ("w", "x", "c"), ("z", "y")
    in_specs = (
        P(ctx, exp),
        P(ctx, None),
        P(ctx, None),
        P(exp, ctx),
        P(exp, None),
        P(exp, None),
        P(exp, ctx, None),
        P(exp, ctx, None),
        P(exp, None, ctx),
    )
    out_specs = (P(ctx, exp), P(exp, ctx))
    return jax.shard_map(body, mesh=fine, in_specs=in_specs, out_specs=out_specs, check_vma=False)
```
